256 devices in a mesh: gx: 16 (over y_hi, z), gy: 8 (over x, core), gz: 2 (over y_lo).
Axes of the slice: x: 4, y: 4 (y_hi: 2, y_lo: 2; y = y_hi * 2 + y_lo), z: 8, core: 2. Of those that a mesh axis runs over, the one named last changes fastest.
Arguments:
- start_field: float32 [3, 128, 192, 256], P(None, 'gx', 'gy', 'gz'), may hold values from -6 to 6
- stiffness: float32 [128, 192, 256], P('gx', 'gy', 'gz'), may hold values from 1 to 10
- mass: float32 [128, 192, 256], P('gx', 'gy', 'gz'), may hold values from 0.5 to 20
- sens_values: float32 [3, 2, 128, 4096], P(None, 'gz', ('gx', 'gy')), may hold values from -48 to 48
- sens_cells: int32 [2, 128, 4096], P('gz', ('gx', 'gy')), may hold values from 0 to 24575
- sens_counts: int32 [2, 128, 128], P('gz', ('gx', 'gy')), may hold values from 0 to 32, as said below
- hull_cells: int32 [16, 16, 4096], P('gx', ('gy', 'gz')), may hold values from 0 to 24575
- hull_patches: int32 [16, 16, 4096], P('gx', ('gy', 'gz')), may hold values from 0 to 262143
Outputs:
- adjoint_field: float32 [3, 128, 192, 256], P(None, 'gx', 'gy', 'gz')
- patch_gradient: float32 [3, 1024, 4096], P(None, ('gy', 'gz'), 'gx')
The draws below stay inside these ranges and needn't reach their ends.
Inputs may be any that keep to these rules, and one draw needn't show every extreme that they name: sens_counts[g, s, j] counts the live slots among the 32 slots that flow partition s of vertical block g sends to mesh block j. Every partition fills some block, and in every vertical block one mesh block receives 32 live slots from every partition.
All inputs are finite; a program needn't handle non-finite values.
Results may differ from the reference program's by a relative error of at most 0.0001.
Values sent between devices are 32-bit elements; how exact they have to be, the bound alone decides.
No kernel may reach another device: no remote copies, remote signals or barrier semaphores. Data moves between devices by JAX's collectives and lax.ppermute only.
A program may use at most 320 MiB of HBM per device.

```python
import math
import jax
import jax.numpy as jnp

CX = 8
CY = 24
CZ = 128
SWEEPS = 3
CAP = 32
HULL = 4096
PROWS_DEV = 256
BLOCKS = 128
NX = 128
NY = 192
NZ = 256
PATCH_ROWS = 4096
PATCH_COLS = 1024
N_GX = 16
N_GY = 8
N_GZ = 2


def draw_sens_counts(key, part):
    key = jax.random.fold_in(key, 11)
    first_key, second_key, third_key = jax.random.split(key, 3)
    counts = jax.random.randint(first_key, (N_GZ, BLOCKS, BLOCKS), 0, CAP + 1)
    columns = jnp.arange(BLOCKS, dtype=jnp.int32)[None, None, :]
    row_full = jax.random.randint(second_key, (N_GZ, BLOCKS, 1), 0, BLOCKS)
    column_full = jax.random.randint(third_key, (N_GZ, 1, 1), 0, BLOCKS)
    filled = (columns == row_full) | (columns == column_full)
    return jnp.where(filled, CAP, counts).astype(jnp.int32)


def with_ends(entries, own_key, low, high):
    longest = entries.shape.index(max(entries.shape))
    spots = []
    for shift in (0, 1):
        where = [jax.random.randint(jax.random.fold_in(own_key, axis), (), 0, length) for axis, length in enumerate(entries.shape)]
        where[longest] = (where[longest] + shift) % entries.shape[longest]
        spots.append(tuple(where))
    return entries.at[spots[0]].set(low).at[spots[1]].set(high)


def block_scale(own_key, dims, cuts, smallest, largest):
    def one(dim, shards_of):
        heights = jax.random.uniform(jax.random.fold_in(jax.random.fold_in(own_key, 6), dim), (shards_of,), jnp.float32, smallest / len(cuts), largest / len(cuts))
        return jnp.repeat(jnp.exp(heights), dims[dim] // shards_of).reshape((-1,) + (1,) * (len(dims) - dim - 1))

    loudness = one(*cuts[0])
    for cut in cuts[1:]:
        loudness = loudness * one(*cut)
    return loudness


def centred(stream_key, extent, width, reach, shards=(), held_as=jnp.bfloat16):
    values = jax.random.normal(stream_key, extent, jnp.float32) * width
    if len(shards) > 0:
        values = block_scale(stream_key, extent, shards, -0.22, 0.18) * values
    return jnp.clip(values, min=-reach, max=reach).astype(held_as)


def setup_inputs(seed: int = 0) -> dict:
    keys = jax.random.split(jax.random.key(seed), 9)
    start_field = centred(keys[0], (3, NX, NY, NZ), 1.0, 6.0, ((1, 16), (2, 8), (3, 2)), jnp.float32)
    stiffness = jnp.clip(jnp.exp(math.log(10.0) - 2.3025851 * jax.random.uniform(keys[1], (NX, NY, NZ), jnp.float32) ** block_scale(keys[1], (NX, NY, NZ), ((0, 16), (1, 8), (2, 2)), -0.2, 0.2)), 1.0, 10.0)
    mass = jnp.clip(jnp.exp(math.log(20.0) - 3.6888795 * jax.random.uniform(keys[2], (NX, NY, NZ), jnp.float32) ** block_scale(keys[2], (NX, NY, NZ), ((0, 16), (1, 8), (2, 2)), -0.2, 0.2)), 0.5, 20.0)
    sens_values = centred(keys[3], (3, N_GZ, BLOCKS, BLOCKS * CAP), 8.0, 48.0, ((1, 2), (2, 128)), jnp.float32)
    sens_cells = with_ends(jax.random.randint(keys[4], (N_GZ, BLOCKS, BLOCKS * CAP), 0, CX * CY * CZ), jax.random.fold_in(keys[4], 1), 0, (CX * CY * CZ) - 1).astype(jnp.int32)
    sens_counts = draw_sens_counts(jax.random.fold_in(keys[8], 71), 0)
    hull_cells = with_ends(jax.random.randint(keys[6], (N_GX, N_GY * N_GZ, HULL), 0, CX * CY * CZ), jax.random.fold_in(keys[6], 1), 0, (CX * CY * CZ) - 1).astype(jnp.int32)
    hull_patches = with_ends(jax.random.randint(keys[7], (N_GX, N_GY * N_GZ, HULL), 0, PATCH_COLS * PROWS_DEV), jax.random.fold_in(keys[7], 1), 0, (PATCH_COLS * PROWS_DEV) - 1).astype(jnp.int32)
    return dict(start_field=start_field, stiffness=stiffness, mass=mass, sens_values=sens_values, sens_cells=sens_cells, sens_counts=sens_counts, hull_cells=hull_cells, hull_patches=hull_patches)


relax_weight = 0.8


def face_cuts():
    middle = slice(1, -1)
    result = []
    for axis_num in range(3):
        for side_cut in (slice(2, None), slice(None, -2)):
            parts = [middle, middle, middle]
            parts[axis_num] = side_cut
            result.append(tuple(parts))
    return result


def relax_sweep(field_rim, stiff_rim, source, mass, inside):
    middle = (slice(1, -1), slice(1, -1), slice(1, -1))
    center = field_rim[(slice(None),) + middle]
    stiff_center = stiff_rim[middle]
    weight_sum = jnp.zeros_like(stiff_center)
    flux_sum = jnp.zeros_like(center)
    for cut in face_cuts():
        weight = 0.5 * (stiff_center + stiff_rim[cut])
        weight_sum = weight_sum + weight
        flux_sum = flux_sum + weight * (center - field_rim[(slice(None),) + cut])
    mass_term = mass * (center + 0.25 * jnp.sum(center, axis=0))
    residual = source - flux_sum - mass_term
    diagonal = weight_sum + 1.25 * mass
    if inside is not None:
        diagonal = jnp.where(inside, diagonal, 1.0)
    updated = center + relax_weight * residual / diagonal
    if inside is not None:
        updated = jnp.where(inside, updated, 0.0)
    return updated


def global_cells(local, block_x, block_y, block_z):
    pos_x = block_x * CX + local // (CY * CZ)
    pos_y = block_y * CY + (local // CZ) % CY
    pos_z = block_z * CZ + local % CZ
    return ((pos_x * NY + pos_y) * NZ + pos_z).astype(jnp.int32)


def reference(start_field, stiffness, mass, sens_values, sens_cells, sens_counts, hull_cells, hull_patches):
    slot_ids = jnp.arange(BLOCKS * CAP, dtype=jnp.int32)
    limits = jnp.repeat(sens_counts, CAP, axis=2)
    live_slots = (slot_ids % CAP)[None, None, :] < limits
    block_ids = slot_ids // CAP
    vertical = jnp.arange(N_GZ, dtype=jnp.int32)[:, None, None]
    target = global_cells(sens_cells, (block_ids // N_GY)[None, None, :], (block_ids % N_GY)[None, None, :], vertical)
    values = jnp.where(live_slots[None], sens_values, 0.0)
    source = jnp.zeros((3, NX * NY * NZ), jnp.float32).at[:, target.reshape(-1)].add(values.reshape(3, -1))
    source = source.reshape(3, NX, NY, NZ)
    stiff_rim = jnp.pad(stiffness, 1)
    field_now = start_field
    for sweep in range(SWEEPS):
        field_rim = jnp.pad(field_now, ((0, 0), (1, 1), (1, 1), (1, 1)))
        field_now = relax_sweep(field_rim, stiff_rim, source, mass, None)
    block_x = jnp.arange(N_GX, dtype=jnp.int32)[:, None, None]
    rest_ids = jnp.arange(N_GY * N_GZ, dtype=jnp.int32)[None, :, None]
    hull_target = global_cells(hull_cells, block_x, rest_ids // N_GZ, rest_ids % N_GZ)
    flat_field = field_now.reshape(3, -1)
    flat_stiff = stiffness.reshape(-1)
    hull_values = flat_field[:, hull_target] * flat_stiff[hull_target]
    girth = hull_patches // PROWS_DEV
    length = block_x * PROWS_DEV + hull_patches % PROWS_DEV
    patch_ids = (girth * PATCH_ROWS + length).astype(jnp.int32)
    patch = jnp.zeros((3, PATCH_COLS * PATCH_ROWS), jnp.float32).at[:, patch_ids.reshape(-1)].add(hull_values.reshape(3, -1))
    return field_now, patch.reshape(3, PATCH_COLS, PATCH_ROWS)
```

```python
import jax
import jax.numpy as jnp
from jax import lax
from jax.experimental import pallas as pl
from jax.experimental.pallas import tpu as pltpu
from jax.sharding import PartitionSpec as P

CX, CY, CZ = 8, 24, 128
LANES = 128
SLOTS = 4096
SLOT_ROWS = SLOTS // LANES
BLOCKS = 128
CAP = 32
HULL_DESTS = 16
PATCH_BLOCK = 64 * 256
HULL_ROWS = 3
HULL_CAP = HULL_ROWS * LANES - 1
Y_ROWS = 20
Y_FIELDS = ((0, 3), (3, 3), (6, 3), (9, 3), (12, 2), (14, 2), (16, 2), (18, 2))
Z_ROWS = 24
EXT_X = CX + 6
EXT_Y = 32
RELAX = 0.8

f32, bf16, i32 = jnp.float32, jnp.bfloat16, jnp.int32
PARAMS = pltpu.CompilerParams(vmem_limit_bytes=56 * 1024 * 1024)


def iota(shape, dim):
    return lax.broadcasted_iota(i32, shape, dim)


def halves(values):
    high = values.astype(bf16).astype(f32)
    return high, values - high


def dot_last(a, b):
    return lax.dot_general(a, b, (((1,), (1,)), ((), ())), preferred_element_type=f32)


def pack_slots(values_ref, cells_ref, counts_ref, out_ref):
    counts = counts_ref[...].astype(f32)
    spread = jnp.where(iota((SLOT_ROWS, BLOCKS), 1) // 4 == iota((SLOT_ROWS, BLOCKS), 0), counts, 0.0)
    place = jnp.where(iota((BLOCKS, LANES), 0) % 4 == iota((BLOCKS, LANES), 1) // CAP, 1.0, 0.0)
    limits = jnp.dot(spread.astype(bf16), place.astype(bf16), preferred_element_type=f32)
    lane = iota((SLOT_ROWS, LANES), 1)
    live = (lane % CAP).astype(f32) < limits
    parts = [jnp.where(live, values_ref[c], 0.0) for c in range(3)] + [cells_ref[...].astype(f32)]
    quarter = lane // CAP
    row = iota((SLOT_ROWS, LANES), 0)
    for q in range(4):
        message = jnp.zeros((SLOT_ROWS, LANES), f32)
        for c in range(4):
            turned = parts[c] if c == q else pltpu.roll(parts[c], (c - q) * CAP % LANES, 1)
            message = jnp.where(quarter == c, turned, message)
        below = jnp.where(row >= 2, pltpu.roll(message, 2, 0), 0.0)
        above = jnp.where(row < SLOT_ROWS - 2, pltpu.roll(message, SLOT_ROWS - 2, 0), 0.0)
        out_ref[pl.ds(3 * q, SLOT_ROWS, stride=12), :] = below
        out_ref[pl.ds(3 * q + 1, SLOT_ROWS, stride=12), :] = message
        out_ref[pl.ds(3 * q + 2, SLOT_ROWS, stride=12), :] = above


def scatter_slots(slots_ref, field_ref, stiff_ref, mass_ref, xlow_ref, xhigh_ref, source_ref, ylow_ref, yhigh_ref, rows_s, lanes_s, left_s, right_s):
    lane = iota((SLOT_ROWS, LANES), 1)
    quarter = lane // CAP
    own_rows = CY * CX
    side_rows = CY * 2

    def unpack(k):
        parts = [jnp.zeros((SLOT_ROWS, LANES), f32) for _ in range(4)]
        for q in range(4):
            message = slots_ref[pl.ds(3 * q + k, SLOT_ROWS, stride=12), :]
            for c in range(4):
                turned = message if c == q else pltpu.roll(message, (q - c) * CAP % LANES, 1)
                parts[c] = jnp.where(quarter == q, turned, parts[c])
        ids = parts[3].astype(i32)
        pieces = []
        for c in range(3):
            pieces.extend(halves(parts[c]))
        return ids // LANES, ids % LANES, pieces

    lane_number = iota((LANES, LANES), 0)
    row_number = iota((own_rows, LANES), 0)
    side_number = iota((side_rows, LANES), 0)
    rows, lanes, pieces = unpack(1)
    for r in range(SLOT_ROWS):
        cut = slice(r * LANES, (r + 1) * LANES)
        rows_s[:, cut] = jnp.where(row_number == rows[r : r + 1, :], 1.0, 0.0).astype(bf16)
        here = lane_number == lanes[r : r + 1, :]
        for n in range(6):
            lanes_s[n * LANES : (n + 1) * LANES, cut] = jnp.where(here, pieces[n][r : r + 1, :], 0.0).astype(bf16)
    sums = dot_last(rows_s[...], lanes_s[...])
    for c in range(3):
        one = sums[:, 2 * c * LANES : (2 * c + 1) * LANES] + sums[:, (2 * c + 1) * LANES : (2 * c + 2) * LANES]
        source_ref[c, 2 : 2 + CX] = one.reshape(CX, CY, LANES)
    for k, first, target in ((0, own_rows - side_rows, 0), (2, 0, 2 + CX)):
        rows, lanes, pieces = unpack(k)
        for r in range(SLOT_ROWS):
            cut = slice(r * LANES, (r + 1) * LANES)
            here = side_number == rows[r : r + 1, :] - first
            for n in range(6):
                left_s[n * side_rows : (n + 1) * side_rows, cut] = jnp.where(here, pieces[n][r : r + 1, :], 0.0).astype(bf16)
            right_s[:, cut] = jnp.where(lane_number == lanes[r : r + 1, :], 1.0, 0.0).astype(bf16)
        sums = dot_last(left_s[...], right_s[...])
        for c in range(3):
            one = sums[2 * c * side_rows : (2 * c + 1) * side_rows] + sums[(2 * c + 1) * side_rows : (2 * c + 2) * side_rows]
            source_ref[c, target : target + 2] = one.reshape(2, CY, LANES)
    for out_ref, low in ((ylow_ref, True), (yhigh_ref, False)):
        for number, (start, width) in enumerate(Y_FIELDS):
            rows = slice(0, width) if low else slice(CY - width, CY)
            here = slice(start, start + width)
            if number >= 5:
                out_ref[:, here, :] = source_ref[number - 5, :, rows, :]
                continue
            if number < 4:
                before, after = slice(3 * number + 1, 3 * number + 3), slice(3 * number, 3 * number + 2)
            else:
                before = after = slice(12, 14)
            own = field_ref.at[number] if number < 3 else (stiff_ref if number == 3 else mass_ref)
            out_ref[0:2, here, :] = xlow_ref[before, rows, :]
            out_ref[2 : 2 + CX, here, :] = own[:, rows, :]
            out_ref[2 + CX :, here, :] = xhigh_ref[after, rows, :]


def route_hull(cells_ref, patches_ref, where_ref, ids_ref, rows_s, lanes_s):
    patches = patches_ref[...]
    cells = cells_ref[...]
    dest = patches // PATCH_BLOCK
    local = patches % PATCH_BLOCK
    hits = [jnp.where(dest == d, 1.0, 0.0) for d in range(HULL_DESTS)]
    stacked = jnp.concatenate(hits, axis=0).astype(bf16)
    upto = jnp.where(iota((LANES, LANES), 0) <= iota((LANES, LANES), 1), 1.0, 0.0).astype(bf16)
    total = HULL_DESTS * SLOT_ROWS
    within = jnp.dot(stacked, upto, preferred_element_type=f32)
    row_sums = jnp.dot(stacked, jnp.ones((LANES, LANES), bf16), preferred_element_type=f32)
    a, b = iota((total, total), 0), iota((total, total), 1)
    earlier = jnp.where((a // SLOT_ROWS == b // SLOT_ROWS) & (b < a), 1.0, 0.0).astype(bf16)
    offsets = jnp.dot(earlier, row_sums.astype(bf16), preferred_element_type=f32)
    rank = jnp.zeros((SLOT_ROWS, LANES), f32)
    for d in range(HULL_DESTS):
        cut = slice(d * SLOT_ROWS, (d + 1) * SLOT_ROWS)
        rank = rank + hits[d] * (within[cut] + offsets[cut] - 1.0)
    rank = rank.astype(i32)
    overflow = jnp.max(jnp.where(rank >= HULL_CAP, 1.0, 0.0))
    slot_row = jnp.where(rank < HULL_CAP, dest * HULL_ROWS + rank // LANES, -1)
    slot_lane = rank % LANES
    payload = [cells // LANES, cells % LANES, local // 256 + 1, local % 256]
    payload = [p.astype(f32) for p in payload]
    count = HULL_DESTS * HULL_ROWS
    row_number = iota((count, LANES), 0)
    lane_number = iota((LANES, LANES), 0)
    for r in range(SLOT_ROWS):
        cut = slice(r * LANES, (r + 1) * LANES)
        here = row_number == slot_row[r : r + 1, :]
        for n in range(4):
            rows_s[n * count : (n + 1) * count, cut] = jnp.where(here, payload[n][r : r + 1, :], 0.0).astype(bf16)
        lanes_s[:, cut] = jnp.where(lane_number == slot_lane[r : r + 1, :], 1.0, 0.0).astype(bf16)
    placed = dot_last(rows_s[...], lanes_s[...])
    where_ref[...] = placed[: 2 * count].astype(i32)
    ids = jnp.maximum((placed[2 * count : 3 * count] - 1.0) * 256.0 + placed[3 * count :] + 1.0, 0.0)
    last = (iota((count, LANES), 1) == LANES - 1) & (row_number % HULL_ROWS == HULL_ROWS - 1)
    ids_ref[...] = jnp.where(last, overflow, ids)


def widen(side_ref, field_ref, stiff_ref, mass_ref, source_ref, xlow_ref, xhigh_ref, ylow_ref, yhigh_ref, ext_ref, z_ref):
    side = side_ref[0]
    lane = iota((1, 1, LANES), 2)
    zeros = jnp.zeros((EXT_X, EXT_Y - CY, LANES), f32)
    total = jnp.zeros((EXT_X - 2, EXT_Y, LANES), f32)
    for number, (start, width) in enumerate(Y_FIELDS):
        target = ext_ref.at[number]
        target[:, CY:, :] = zeros
        if number >= 5:
            target[1 : EXT_X - 1, :CY, :] = source_ref[number - 5]
            target[0, :CY, :] = jnp.zeros((CY, LANES), f32)
            target[EXT_X - 1, :CY, :] = jnp.zeros((CY, LANES), f32)
        elif number == 4:
            target[0, :CY, :] = jnp.zeros((CY, LANES), f32)
            target[EXT_X - 1, :CY, :] = jnp.zeros((CY, LANES), f32)
            target[1:3, :CY, :] = xlow_ref[12:14]
            target[3 : 3 + CX, :CY, :] = mass_ref[...]
            target[3 + CX : 5 + CX, :CY, :] = xhigh_ref[12:14]
        else:
            own = field_ref.at[number] if number < 3 else stiff_ref
            target[0:3, :CY, :] = xlow_ref[3 * number : 3 * number + 3]
            target[3 : 3 + CX, :CY, :] = own[...]
            target[3 + CX :, :CY, :] = xhigh_ref[3 * number : 3 * number + 3]
        target[1 : EXT_X - 1, CY : CY + width, :] = yhigh_ref[:, start : start + width, :]
        target[1 : EXT_X - 1, EXT_Y - width :, :] = ylow_ref[:, start : start + width, :]
        shift = jnp.where(side == 0, (3 * number + 3) % LANES, 3 * number)
        turned = pltpu.roll(target[1 : EXT_X - 1].reshape((EXT_X - 2) * EXT_Y, LANES), shift, 1)
        turned = turned.reshape(EXT_X - 2, EXT_Y, LANES)
        total = jnp.where((lane >= 3 * number) & (lane < 3 * number + 3), turned, total)
    flipped = jnp.transpose(total.reshape((EXT_X - 2) * EXT_Y, LANES))
    z_ref[...] = flipped[:Z_ROWS]


def relax_and_gather(
    side_ref, ext_ref, z_ref, where_ref, ids_ref, out_ref, message_ref, first_s, second_s, stiff_s, weight_s, keep_s, couple_s, push_s, turned_s
):
    side = side_ref[0]
    wide = 2 * LANES
    rows = (EXT_X - 2) * EXT_Y
    lane = iota((1, 1, LANES), 2)
    padded = jnp.concatenate([z_ref[...], jnp.zeros((LANES - Z_ROWS, rows), f32)], axis=0)
    columns = jnp.transpose(padded)
    first_lane = jnp.where(side == 0, 0, LANES - 3)
    near = (lane >= first_lane) & (lane < first_lane + 3)

    def beyond(number):
        shift = jnp.where(side == 0, (LANES - 3 * number) % LANES, (2 * LANES - 3 - 3 * number) % LANES)
        return jnp.where(near, pltpu.roll(columns, shift, 1).reshape(EXT_X - 2, EXT_Y, LANES), 0.0)

    empty = jnp.zeros((EXT_Y, LANES), f32)
    for c in range(3):
        first_s[c, :, :, :LANES] = ext_ref[c]
        first_s[c, 1 : EXT_X - 1, :, LANES:] = beyond(c)
        first_s[c, 0, :, LANES:] = empty
        first_s[c, EXT_X - 1, :, LANES:] = empty
    stiff_s[:, :, :LANES] = ext_ref[3]
    stiff_s[1 : EXT_X - 1, :, LANES:] = beyond(3)
    stiff_s[0, :, LANES:] = empty
    stiff_s[EXT_X - 1, :, LANES:] = empty
    keep_s[:, :, :LANES] = ext_ref[4, 1 : EXT_X - 1]
    keep_s[:, :, LANES:] = beyond(4)
    for c in range(3):
        push_s[c, :, :, :LANES] = ext_ref[5 + c, 1 : EXT_X - 1]
        push_s[c, :, :, LANES:] = beyond(5 + c)

    def around(ref_at, x):
        middle = ref_at(x)
        return middle, (
            ref_at(x + 1),
            ref_at(x - 1),
            pltpu.roll(middle, EXT_Y - 1, 0),
            pltpu.roll(middle, 1, 0),
            pltpu.roll(middle, wide - 1, 1),
            pltpu.roll(middle, 1, 1),
        )

    def prepare(i, carry):
        middle, others = around(lambda x: stiff_s[x], i + 1)
        weights = [0.5 * (middle + other) for other in others]
        weight_sum = weights[0] + weights[1] + weights[2] + weights[3] + weights[4] + weights[5]
        mass = keep_s[i]
        inside = middle > 0.0
        rate = jnp.where(inside, RELAX / jnp.where(inside, weight_sum + 1.25 * mass, 1.0), 0.0)
        for n in range(6):
            weight_s[n, i] = rate * weights[n]
        keep_s[i] = jnp.where(inside, 1.0 - rate * (weight_sum + mass), 0.0)
        couple_s[i] = 0.25 * rate * mass
        for c in range(3):
            push_s[c, i] = rate * push_s[c, i]
        return carry

    lax.fori_loop(0, EXT_X - 2, prepare, 0)

    def sweep(source, target, lowest, highest):
        def one(x, carry):
            i = x - 1
            gathered = [around(lambda y, c=c: source[c, y], x) for c in range(3)]
            shared = couple_s[i] * (gathered[0][0] + gathered[1][0] + gathered[2][0])
            for c in range(3):
                middle, others = gathered[c]
                value = keep_s[i] * middle + (push_s[c, i] - shared)
                for n in range(6):
                    value = value + weight_s[n, i] * others[n]
                target[c, x] = value
            return carry

        lax.fori_loop(lowest, highest, one, 0)

    sweep(first_s, second_s, 1, EXT_X - 1)
    sweep(second_s, first_s, 2, EXT_X - 2)
    sweep(first_s, second_s, 3, EXT_X - 3)

    own_rows = CX * CY
    blank = jnp.zeros((2 * LANES - own_rows, LANES), f32)
    for c in range(3):
        result = second_s[c, 3 : 3 + CX, :CY, :LANES]
        out_ref[c] = result
        scaled = (result * stiff_s[3 : 3 + CX, :CY, :LANES]).reshape(own_rows, LANES)
        high, low = halves(scaled)
        cut = slice(c * LANES, (c + 1) * LANES)
        turned_s[cut, : 2 * LANES] = jnp.transpose(jnp.concatenate([high, blank], axis=0)).astype(bf16)
        turned_s[cut, 2 * LANES :] = jnp.transpose(jnp.concatenate([low, blank], axis=0)).astype(bf16)
    count = HULL_DESTS * HULL_ROWS
    row_number = iota((2 * LANES, LANES), 0)
    lane_number = iota((LANES, LANES), 0)
    for d in range(HULL_DESTS):
        chosen = []
        for i in range(HULL_ROWS):
            r = d * HULL_ROWS + i
            chosen.append(jnp.where(row_number == where_ref[r : r + 1, :], 1.0, 0.0).astype(bf16))
        chosen = jnp.concatenate(chosen, axis=1)
        found = jnp.dot(turned_s[...], jnp.concatenate([chosen, chosen], axis=0), preferred_element_type=f32)
        for i in range(HULL_ROWS):
            r = d * HULL_ROWS + i
            here = lane_number == where_ref[count + r : count + r + 1, :]
            for c in range(3):
                part = found[c * LANES : (c + 1) * LANES, i * LANES : (i + 1) * LANES]
                value = jnp.sum(jnp.where(here, part, 0.0), axis=0, keepdims=True)
                spot = d * 4 * HULL_ROWS + c * HULL_ROWS + i
                message_ref[spot : spot + 1, :] = value
            spot = d * 4 * HULL_ROWS + 3 * HULL_ROWS + i
            message_ref[spot : spot + 1, :] = ids_ref[r : r + 1, :]


def scatter_hull(nodes_ref, out_ref):
    row_number = iota((64, LANES), 0)
    column_number = iota((256, LANES), 0)
    sums = jnp.zeros((6 * 64, 256), f32)
    for s in range(HULL_DESTS):
        lefts, rights = [], []
        for i in range(HULL_ROWS):
            base = s * 4 * HULL_ROWS + i
            ids = nodes_ref[base + 3 * HULL_ROWS : base + 3 * HULL_ROWS + 1, :].astype(i32) - 1
            here = row_number == (ids >> 8)
            pieces = []
            for c in range(3):
                values = nodes_ref[base + c * HULL_ROWS : base + c * HULL_ROWS + 1, :]
                pieces.extend(jnp.where(here, part, 0.0).astype(bf16) for part in halves(values))
            lefts.append(jnp.concatenate(pieces, axis=0))
            rights.append(jnp.where(column_number == (ids & 255), 1.0, 0.0).astype(bf16))
        sums = sums + dot_last(jnp.concatenate(lefts, axis=1), jnp.concatenate(rights, axis=1))
    for c in range(3):
        out_ref[c] = sums[2 * c * 64 : (2 * c + 1) * 64] + sums[(2 * c + 1) * 64 : (2 * c + 2) * 64]


def shaped(*shape, dtype=f32):
    return jax.ShapeDtypeStruct(shape, dtype)


def call(kernel, outs, scratch, cost, *args, scalars=0):
    specs = [pl.BlockSpec(memory_space=pltpu.SMEM)] * scalars + [pl.BlockSpec(memory_space=pltpu.VMEM)] * (len(args) - scalars)
    many = isinstance(outs, tuple)
    vmem = pl.BlockSpec(memory_space=pltpu.VMEM)
    return pl.pallas_call(
        kernel,
        out_shape=outs,
        in_specs=specs,
        out_specs=tuple(vmem for _ in outs) if many else vmem,
        scratch_shapes=[pltpu.VMEM(shape, dtype) for shape, dtype in scratch],
        compiler_params=PARAMS,
        cost_estimate=pl.CostEstimate(flops=cost, bytes_accessed=1 << 20, transcendentals=0),
        name=kernel.__name__,
    )(*args)


def step(axis, values, up):
    count = lax.axis_size(axis)
    pairs = [(i, i + 1) if up else (i + 1, i) for i in range(count - 1)]
    return lax.ppermute(values, axis, pairs)


def per_device(start_field, stiffness, mass, sens_values, sens_cells, sens_counts, hull_cells, hull_patches):
    last = jnp.concatenate([start_field[:, CX - 3 :].reshape(9, CY, CZ), stiffness[CX - 3 :], mass[CX - 2 :]], axis=0)
    first = jnp.concatenate([start_field[:, :3].reshape(9, CY, CZ), stiffness[:3], mass[:2]], axis=0)
    xlow = step("gx", last, True)
    xhigh = step("gx", first, False)
    packed = call(
        pack_slots,
        shaped(3 * BLOCKS, LANES),
        [],
        1 << 20,
        sens_values.reshape(3, SLOT_ROWS, LANES),
        sens_cells.reshape(SLOT_ROWS, LANES),
        sens_counts.reshape(1, BLOCKS),
    )
    arrived = lax.all_to_all(packed, ("gx", "gy"), split_axis=0, concat_axis=0, tiled=True)
    source, first_rows, last_rows = call(
        scatter_slots,
        (shaped(3, CX + 4, CY, CZ), shaped(CX + 4, Y_ROWS, CZ), shaped(CX + 4, Y_ROWS, CZ)),
        [((CX * CY, SLOTS), bf16), ((6 * LANES, SLOTS), bf16), ((12 * CY, SLOTS), bf16), ((LANES, SLOTS), bf16)],
        1 << 32,
        arrived,
        start_field,
        stiffness,
        mass,
        xlow,
        xhigh,
    )
    ylow = step("gy", last_rows, True)
    yhigh = step("gy", first_rows, False)
    count = HULL_DESTS * HULL_ROWS
    where, ids = call(
        route_hull,
        (shaped(2 * count, LANES, dtype=i32), shaped(count, LANES)),
        [((4 * count, SLOTS), bf16), ((LANES, SLOTS), bf16)],
        1 << 31,
        hull_cells.reshape(SLOT_ROWS, LANES),
        hull_patches.reshape(SLOT_ROWS, LANES),
    )
    side = lax.axis_index("gz").astype(i32).reshape(1)
    rows = (EXT_X - 2) * EXT_Y
    ext, faces = call(
        widen,
        (shaped(8, EXT_X, EXT_Y, CZ), shaped(Z_ROWS, rows)),
        [],
        1 << 20,
        side,
        start_field,
        stiffness,
        mass,
        source,
        xlow,
        xhigh,
        ylow,
        yhigh,
        scalars=1,
    )
    faces = lax.ppermute(faces, "gz", [(0, 1), (1, 0)])
    wide = (EXT_X - 2, EXT_Y, 2 * CZ)
    full = (EXT_X, EXT_Y, 2 * CZ)
    field, outgoing = call(
        relax_and_gather,
        (shaped(3, CX, CY, CZ), shaped(4 * count, LANES)),
        [
            ((3,) + full, f32),
            ((3,) + full, f32),
            (full, f32),
            ((6,) + wide, f32),
            (wide, f32),
            (wide, f32),
            ((3,) + wide, f32),
            ((3 * LANES, 4 * LANES), bf16),
        ],
        1 << 32,
        side,
        ext,
        faces,
        where,
        ids,
        scalars=1,
    )
    nodes = lax.all_to_all(outgoing, ("gy", "gz"), split_axis=0, concat_axis=0, tiled=True)
    overflow = jnp.max(nodes.reshape(HULL_DESTS, 4 * HULL_ROWS, LANES)[:, -1, -1])

    def in_messages():
        return call(scatter_hull, shaped(3, 64, 256), [], 1 << 32, nodes)

    def every_node():
        cells = hull_cells[0, 0]
        values = field.reshape(3, -1)[:, cells] * stiffness.reshape(-1)[cells]
        sent = jnp.concatenate([values, hull_patches[0].astype(f32)], axis=0)
        sent = jnp.broadcast_to(sent[None], (HULL_DESTS,) + sent.shape)
        got = lax.all_to_all(sent, ("gy", "gz"), split_axis=0, concat_axis=0, tiled=True)
        got = jnp.swapaxes(got, 0, 1).reshape(4, -1)
        spots = got[3].astype(i32) - lax.axis_index(("gy", "gz")) * PATCH_BLOCK
        mine = (spots >= 0) & (spots < PATCH_BLOCK)
        added = jnp.where(mine, got[:3], 0.0)
        patch = jnp.zeros((3, PATCH_BLOCK), f32).at[:, jnp.where(mine, spots, 0)].add(added)
        return patch.reshape(3, 64, 256)

    patch = lax.cond(overflow > 0.0, every_node, in_messages)
    return field, patch


def solution(mesh):
    placed = (
        P(None, "gx", "gy", "gz"),
        P("gx", "gy", "gz"),
        P("gx", "gy", "gz"),
        P(None, "gz", ("gx", "gy"), None),
        P("gz", ("gx", "gy"), None),
        P("gz", ("gx", "gy"), None),
        P("gx", ("gy", "gz"), None),
        P("gx", ("gy", "gz"), None),
    )
    return jax.shard_map(
        per_device,
        mesh=mesh,
        in_specs=placed,
        out_specs=(P(None, "gx", "gy", "gz"), P(None, ("gy", "gz"), "gx")),
        check_vma=False,
    )
```

```python
import functools

import jax
import jax.numpy as jnp
from jax import lax
from jax.experimental import pallas as pl
from jax.experimental.pallas import tpu as pltpu
from jax.sharding import PartitionSpec as P

CX, CY, CZ = 8, 24, 128
LANES = 128
SLOTS = 4096
SLOT_ROWS = SLOTS // LANES
BLOCKS = 128
CAP = 32
HULL_DESTS = 16
PATCH_BLOCK = 64 * 256
HULL_ROWS = 3
HULL_CAP = HULL_ROWS * LANES - 1
Y_ROWS = 20
Y_FIELDS = ((0, 3), (3, 3), (6, 3), (9, 3), (12, 2), (14, 2), (16, 2), (18, 2))
Z_ROWS = 24
EXT_X = CX + 6
EXT_Y = 32
RELAX = 0.8

f32, bf16, i32 = jnp.float32, jnp.bfloat16, jnp.int32
PARAMS = pltpu.CompilerParams(vmem_limit_bytes=24 * 1024 * 1024)


def iota(shape, dim):
    return lax.broadcasted_iota(i32, shape, dim)


def halves(values):
    high = values.astype(bf16).astype(f32)
    return high, values - high


def dot_last(a, b):
    return lax.dot_general(a, b, (((1,), (1,)), ((), ())), preferred_element_type=f32)


def pack_slots(
    gx_ref, values_hbm, cells_hbm, counts_hbm, field_hbm, stiff_hbm, mass_hbm, out_ref, even_ref, odd_ref, values_ref, cells_ref, counts_ref, sems
):
    copies = [
        pltpu.make_async_copy(values_hbm, values_ref, sems.at[0]),
        pltpu.make_async_copy(cells_hbm, cells_ref, sems.at[1]),
        pltpu.make_async_copy(counts_hbm, counts_ref, sems.at[2]),
    ]
    odd = lax.rem(gx_ref[0], 2)
    for slab, up in ((even_ref, 1 - odd), (odd_ref, odd)):
        planes, mass_planes = pl.ds(up * (CX - 3), 3), pl.ds(up * (CX - 2), 2)
        for c in range(3):
            copies.append(pltpu.make_async_copy(field_hbm.at[c, planes], slab.at[pl.ds(3 * c, 3)], sems.at[len(copies)]))
        copies.append(pltpu.make_async_copy(stiff_hbm.at[planes], slab.at[pl.ds(9, 3)], sems.at[len(copies)]))
        copies.append(pltpu.make_async_copy(mass_hbm.at[mass_planes], slab.at[pl.ds(12, 2)], sems.at[len(copies)]))
    for copy in copies:
        copy.start()
    for copy in copies[:3]:
        copy.wait()
    counts = counts_ref[...].astype(f32)
    spread = jnp.where(iota((SLOT_ROWS, BLOCKS), 1) // 4 == iota((SLOT_ROWS, BLOCKS), 0), counts, 0.0)
    place = jnp.where(iota((BLOCKS, LANES), 0) % 4 == iota((BLOCKS, LANES), 1) // CAP, 1.0, 0.0)
    limits = jnp.dot(spread.astype(bf16), place.astype(bf16), preferred_element_type=f32)
    lane = iota((SLOT_ROWS, LANES), 1)
    live = (lane % CAP).astype(f32) < limits
    parts = [jnp.where(live, values_ref[c], 0.0) for c in range(3)] + [cells_ref[...].astype(f32)]
    quarter = lane // CAP
    row = iota((SLOT_ROWS, LANES), 0)
    for q in range(4):
        message = jnp.zeros((SLOT_ROWS, LANES), f32)
        for c in range(4):
            turned = parts[c] if c == q else pltpu.roll(parts[c], (c - q) * CAP % LANES, 1)
            message = jnp.where(quarter == c, turned, message)
        below = jnp.where(row >= 2, pltpu.roll(message, 2, 0), 0.0)
        above = jnp.where(row < SLOT_ROWS - 2, pltpu.roll(message, SLOT_ROWS - 2, 0), 0.0)
        out_ref[pl.ds(3 * q, SLOT_ROWS, stride=12), :] = below
        out_ref[pl.ds(3 * q + 1, SLOT_ROWS, stride=12), :] = message
        out_ref[pl.ds(3 * q + 2, SLOT_ROWS, stride=12), :] = above
    for copy in copies[3:]:
        copy.wait()


def scatter_slots(slots_ref, source_ref, rows_s, lanes_s, left_s, right_s):
    lane = iota((SLOT_ROWS, LANES), 1)
    quarter = lane // CAP
    own_rows = CY * CX
    side_rows = CY * 2

    def unpack(k):
        parts = [jnp.zeros((SLOT_ROWS, LANES), f32) for _ in range(4)]
        for q in range(4):
            message = slots_ref[pl.ds(3 * q + k, SLOT_ROWS, stride=12), :]
            for c in range(4):
                turned = message if c == q else pltpu.roll(message, (q - c) * CAP % LANES, 1)
                parts[c] = jnp.where(quarter == q, turned, parts[c])
        ids = parts[3].astype(i32)
        pieces = []
        for c in range(3):
            pieces.extend(halves(parts[c]))
        return ids // LANES, ids % LANES, pieces

    lane_number = iota((LANES, LANES), 0)
    row_number = iota((2 * LANES, LANES), 0)
    side_number = iota((side_rows, LANES), 0)
    rows, lanes, pieces = unpack(1)
    for r in range(SLOT_ROWS):
        cut = slice(r * LANES, (r + 1) * LANES)
        rows_s[:, cut] = jnp.where(row_number == rows[r : r + 1, :], 1.0, 0.0).astype(bf16)
        here = lane_number == lanes[r : r + 1, :]
        for n in range(6):
            lanes_s[n * LANES : (n + 1) * LANES, cut] = jnp.where(here, pieces[n][r : r + 1, :], 0.0).astype(bf16)
    sums = dot_last(lanes_s[...], rows_s[...])
    for c in range(3):
        one = sums[2 * c * LANES : (2 * c + 1) * LANES] + sums[(2 * c + 1) * LANES : (2 * c + 2) * LANES]
        source_ref[c, 2 : 2 + CX] = jnp.transpose(one)[:own_rows].reshape(CX, CY, LANES)
    for k, first, target in ((0, own_rows - side_rows, 0), (2, 0, 2 + CX)):
        rows, lanes, pieces = unpack(k)
        for r in range(SLOT_ROWS):
            cut = slice(r * LANES, (r + 1) * LANES)
            here = side_number == rows[r : r + 1, :] - first
            for n in range(6):
                left_s[n * side_rows : (n + 1) * side_rows, cut] = jnp.where(here, pieces[n][r : r + 1, :], 0.0).astype(bf16)
            right_s[:, cut] = jnp.where(lane_number == lanes[r : r + 1, :], 1.0, 0.0).astype(bf16)
        sums = dot_last(left_s[...], right_s[...])
        for c in range(3):
            one = sums[2 * c * side_rows : (2 * c + 1) * side_rows] + sums[(2 * c + 1) * side_rows : (2 * c + 2) * side_rows]
            source_ref[c, target : target + 2] = one.reshape(2, CY, LANES)


def by_parity(place, even, odd):
    index, count = place
    is_odd = lax.rem(index, 2) == 1
    low = jnp.where(is_odd, even, odd) * jnp.where(index > 0, 1.0, 0.0)
    high = jnp.where(is_odd, odd, even) * jnp.where(index < count - 1, 1.0, 0.0)
    return low, high


def pack_y(n_gx, gx_ref, gy_ref, source_ref, field_ref, stiff_ref, mass_ref, xeven_ref, xodd_ref, even_ref, odd_ref):
    is_odd = lax.rem(gy_ref[0], 2) == 1
    for number, (start, width) in enumerate(Y_FIELDS):
        here = slice(start, start + width)
        ends = slice(0, width), slice(CY - width, CY)
        pieces = [[], []]
        for n, rows in enumerate(ends):
            if number >= 5:
                pieces[n].append((slice(0, CX + 4), source_ref[number - 5, :, rows, :]))
                continue
            planes = slice(3 * number, 3 * number + 3) if number < 4 else slice(12, 14)
            low, high = by_parity((gx_ref[0], n_gx), xeven_ref[planes, rows, :], xodd_ref[planes, rows, :])
            own = field_ref[number, :, rows, :] if number < 3 else (stiff_ref if number == 3 else mass_ref)[:, rows, :]
            pieces[n].extend([(slice(0, 2), low[-2:]), (slice(2, 2 + CX), own), (slice(2 + CX, CX + 4), high[:2])])
        for (where, first), (_, last) in zip(*pieces):
            even_ref[where, here, :] = jnp.where(is_odd, first, last)
            odd_ref[where, here, :] = jnp.where(is_odd, last, first)


def route_hull(cells_ref, patches_ref, where_ref, ids_ref, rows_s, lanes_s):
    patches = patches_ref[...]
    cells = cells_ref[...]
    dest = patches // PATCH_BLOCK
    local = patches % PATCH_BLOCK
    hits = [jnp.where(dest == d, 1.0, 0.0) for d in range(HULL_DESTS)]
    stacked = jnp.concatenate(hits, axis=0).astype(bf16)
    upto = jnp.where(iota((LANES, LANES), 0) <= iota((LANES, LANES), 1), 1.0, 0.0).astype(bf16)
    total = HULL_DESTS * SLOT_ROWS
    within = jnp.dot(stacked, upto, preferred_element_type=f32)
    row_sums = jnp.dot(stacked, jnp.ones((LANES, LANES), bf16), preferred_element_type=f32)
    a, b = iota((total, total), 0), iota((total, total), 1)
    earlier = jnp.where((a // SLOT_ROWS == b // SLOT_ROWS) & (b < a), 1.0, 0.0).astype(bf16)
    offsets = jnp.dot(earlier, row_sums.astype(bf16), preferred_element_type=f32)
    rank = jnp.zeros((SLOT_ROWS, LANES), f32)
    for d in range(HULL_DESTS):
        cut = slice(d * SLOT_ROWS, (d + 1) * SLOT_ROWS)
        rank = rank + hits[d] * (within[cut] + offsets[cut] - 1.0)
    rank = rank.astype(i32)
    overflow = jnp.max(jnp.where(rank >= HULL_CAP, 1.0, 0.0))
    slot_row = jnp.where(rank < HULL_CAP, dest * HULL_ROWS + rank // LANES, -1)
    slot_lane = rank % LANES
    payload = [cells // LANES, cells % LANES, local // 256 + 1, local % 256]
    payload = [p.astype(f32) for p in payload]
    count = HULL_DESTS * HULL_ROWS
    row_number = iota((count, LANES), 0)
    lane_number = iota((LANES, LANES), 0)
    for r in range(SLOT_ROWS):
        cut = slice(r * LANES, (r + 1) * LANES)
        here = row_number == slot_row[r : r + 1, :]
        for n in range(4):
            rows_s[n * count : (n + 1) * count, cut] = jnp.where(here, payload[n][r : r + 1, :], 0.0).astype(bf16)
        lanes_s[:, cut] = jnp.where(lane_number == slot_lane[r : r + 1, :], 1.0, 0.0).astype(bf16)
    placed = dot_last(rows_s[...], lanes_s[...])
    where_ref[...] = placed[: 2 * count].astype(i32)
    ids = jnp.maximum((placed[2 * count : 3 * count] - 1.0) * 256.0 + placed[3 * count :] + 1.0, 0.0)
    last = (iota((count, LANES), 1) == LANES - 1) & (row_number % HULL_ROWS == HULL_ROWS - 1)
    ids_ref[...] = jnp.where(last, overflow, ids)


def widen(n_gx, n_gy, gx_ref, gy_ref, side_ref, field_ref, stiff_ref, mass_ref, source_ref, xeven_ref, xodd_ref, yeven_ref, yodd_ref, ext_ref, z_ref):
    side = side_ref[0]
    lane = iota((1, 1, LANES), 2)
    zeros = jnp.zeros((EXT_X, EXT_Y - CY, LANES), f32)
    total = jnp.zeros((EXT_X - 2, EXT_Y, LANES), f32)
    for number, (start, width) in enumerate(Y_FIELDS):
        target = ext_ref.at[number]
        target[:, CY:, :] = zeros
        if number >= 5:
            target[1 : EXT_X - 1, :CY, :] = source_ref[number - 5]
            target[0, :CY, :] = jnp.zeros((CY, LANES), f32)
            target[EXT_X - 1, :CY, :] = jnp.zeros((CY, LANES), f32)
        elif number == 4:
            target[0, :CY, :] = jnp.zeros((CY, LANES), f32)
            target[EXT_X - 1, :CY, :] = jnp.zeros((CY, LANES), f32)
            low, high = by_parity((gx_ref[0], n_gx), xeven_ref[12:14], xodd_ref[12:14])
            target[1:3, :CY, :] = low
            target[3 : 3 + CX, :CY, :] = mass_ref[...]
            target[3 + CX : 5 + CX, :CY, :] = high
        else:
            own = field_ref.at[number] if number < 3 else stiff_ref
            planes = slice(3 * number, 3 * number + 3)
            low, high = by_parity((gx_ref[0], n_gx), xeven_ref[planes], xodd_ref[planes])
            target[0:3, :CY, :] = low
            target[3 : 3 + CX, :CY, :] = own[...]
            target[3 + CX :, :CY, :] = high
        here = slice(start, start + width)
        low, high = by_parity((gy_ref[0], n_gy), yeven_ref[:, here, :], yodd_ref[:, here, :])
        target[1 : EXT_X - 1, CY : CY + width, :] = high
        target[1 : EXT_X - 1, EXT_Y - width :, :] = low
        shift = jnp.where(side == 0, (3 * number + 3) % LANES, 3 * number)
        turned = pltpu.roll(target[1 : EXT_X - 1].reshape((EXT_X - 2) * EXT_Y, LANES), shift, 1)
        turned = turned.reshape(EXT_X - 2, EXT_Y, LANES)
        total = jnp.where((lane >= 3 * number) & (lane < 3 * number + 3), turned, total)
    flipped = jnp.transpose(total.reshape((EXT_X - 2) * EXT_Y, LANES))
    z_ref[...] = flipped[:Z_ROWS]


def relax_and_gather(
    side_ref, ext_ref, z_ref, where_ref, ids_ref, out_ref, message_ref, first_s, second_s, stiff_s, weight_s, keep_s, couple_s, push_s, turned_s
):
    side = side_ref[0]
    wide = 2 * LANES
    rows = (EXT_X - 2) * EXT_Y
    lane = iota((1, 1, LANES), 2)
    padded = jnp.concatenate([z_ref[...], jnp.zeros((LANES - Z_ROWS, rows), f32)], axis=0)
    columns = jnp.transpose(padded)
    first_lane = jnp.where(side == 0, 0, LANES - 3)
    near = (lane >= first_lane) & (lane < first_lane + 3)

    def beyond(number):
        shift = jnp.where(side == 0, (LANES - 3 * number) % LANES, (2 * LANES - 3 - 3 * number) % LANES)
        return jnp.where(near, pltpu.roll(columns, shift, 1).reshape(EXT_X - 2, EXT_Y, LANES), 0.0)

    empty = jnp.zeros((EXT_Y, LANES), f32)
    for c in range(3):
        first_s[c, :, :, :LANES] = ext_ref[c]
        first_s[c, 1 : EXT_X - 1, :, LANES:] = beyond(c)
        first_s[c, 0, :, LANES:] = empty
        first_s[c, EXT_X - 1, :, LANES:] = empty
    stiff_s[:, :, :LANES] = ext_ref[3]
    stiff_s[1 : EXT_X - 1, :, LANES:] = beyond(3)
    stiff_s[0, :, LANES:] = empty
    stiff_s[EXT_X - 1, :, LANES:] = empty
    keep_s[:, :, :LANES] = ext_ref[4, 1 : EXT_X - 1]
    keep_s[:, :, LANES:] = beyond(4)
    for c in range(3):
        push_s[c, :, :, :LANES] = ext_ref[5 + c, 1 : EXT_X - 1]
        push_s[c, :, :, LANES:] = beyond(5 + c)

    def around(ref_at, x):
        middle = ref_at(x)
        return middle, (
            ref_at(x + 1),
            ref_at(x - 1),
            pltpu.roll(middle, EXT_Y - 1, 0),
            pltpu.roll(middle, 1, 0),
            pltpu.roll(middle, wide - 1, 1),
            pltpu.roll(middle, 1, 1),
        )

    def prepare(i, carry):
        middle, others = around(lambda x: stiff_s[x], i + 1)
        weights = [0.5 * (middle + other) for other in others]
        weight_sum = weights[0] + weights[1] + weights[2] + weights[3] + weights[4] + weights[5]
        mass = keep_s[i]
        inside = middle > 0.0
        rate = jnp.where(inside, RELAX / jnp.where(inside, weight_sum + 1.25 * mass, 1.0), 0.0)
        for n in range(6):
            weight_s[n, i] = rate * weights[n]
        keep_s[i] = jnp.where(inside, 1.0 - rate * (weight_sum + mass), 0.0)
        couple_s[i] = 0.25 * rate * mass
        for c in range(3):
            push_s[c, i] = rate * push_s[c, i]
        return carry

    lax.fori_loop(0, EXT_X - 2, prepare, 0)

    def sweep(source, target, lowest, highest):
        def one(x, carry):
            i = x - 1
            gathered = [around(lambda y, c=c: source[c, y], x) for c in range(3)]
            shared = couple_s[i] * (gathered[0][0] + gathered[1][0] + gathered[2][0])
            for c in range(3):
                middle, others = gathered[c]
                value = keep_s[i] * middle + (push_s[c, i] - shared)
                for n in range(6):
                    value = value + weight_s[n, i] * others[n]
                target[c, x] = value
            return carry

        lax.fori_loop(lowest, highest, one, 0)

    sweep(first_s, second_s, 1, EXT_X - 1)
    sweep(second_s, first_s, 2, EXT_X - 2)

    def finish(x, carry):
        i = x - 1
        middles = [first_s[c, x, :CY, :LANES] for c in range(3)]
        shared = couple_s[i, :CY, :LANES] * (middles[0] + middles[1] + middles[2])
        for c in range(3):
            columns = first_s[c, x, :, :LANES]
            halo = first_s[c, x, :CY, LANES:]
            others = (
                first_s[c, x + 1, :CY, :LANES],
                first_s[c, x - 1, :CY, :LANES],
                pltpu.roll(columns, EXT_Y - 1, 0)[:CY],
                pltpu.roll(columns, 1, 0)[:CY],
                pltpu.roll(jnp.where(last_lane == 0, halo, middles[c]), LANES - 1, 1),
                pltpu.roll(jnp.where(last_lane == LANES - 1, halo, middles[c]), 1, 1),
            )
            value = keep_s[i, :CY, :LANES] * middles[c] + (push_s[c, i, :CY, :LANES] - shared)
            for n in range(6):
                value = value + weight_s[n, i, :CY, :LANES] * others[n]
            out_ref[c, x - 3] = value
        return carry

    last_lane = iota((CY, LANES), 1)
    lax.fori_loop(3, 3 + CX, finish, 0)

    own_rows = CX * CY
    blank = jnp.zeros((2 * LANES - own_rows, LANES), f32)
    for c in range(3):
        result = out_ref[c]
        scaled = (result * stiff_s[3 : 3 + CX, :CY, :LANES]).reshape(own_rows, LANES)
        high, low = halves(scaled)
        cut = slice(c * LANES, (c + 1) * LANES)
        turned_s[cut, : 2 * LANES] = jnp.transpose(jnp.concatenate([high, blank], axis=0)).astype(bf16)
        turned_s[cut, 2 * LANES :] = jnp.transpose(jnp.concatenate([low, blank], axis=0)).astype(bf16)
    count = HULL_DESTS * HULL_ROWS
    row_number = iota((2 * LANES, LANES), 0)
    lane_number = iota((LANES, LANES), 0)
    group = 2 * HULL_ROWS
    for g in range(count // group):
        chosen = []
        for i in range(group):
            r = g * group + i
            chosen.append(jnp.where(row_number == where_ref[r : r + 1, :], 1.0, 0.0).astype(bf16))
        chosen = jnp.concatenate(chosen, axis=1)
        found = jnp.dot(turned_s[...], jnp.concatenate([chosen, chosen], axis=0), preferred_element_type=f32)
        for i in range(group):
            r = g * group + i
            here = lane_number == where_ref[count + r : count + r + 1, :]
            base = r // HULL_ROWS * 4 * HULL_ROWS + r % HULL_ROWS
            for c in range(3):
                part = found[c * LANES : (c + 1) * LANES, i * LANES : (i + 1) * LANES]
                spot = base + c * HULL_ROWS
                message_ref[spot : spot + 1, :] = jnp.sum(jnp.where(here, part, 0.0), axis=0, keepdims=True)
            spot = base + 3 * HULL_ROWS
            message_ref[spot : spot + 1, :] = ids_ref[r : r + 1, :]


def scatter_hull(nodes_ref, out_hbm, overflow_ref, out_ref, sem):
    flags = nodes_ref[pl.ds(4 * HULL_ROWS - 1, HULL_DESTS, stride=4 * HULL_ROWS), :]
    last = iota((HULL_DESTS, LANES), 1) == LANES - 1
    overflow_ref[0] = jnp.max(jnp.where(last, flags, 0.0)).astype(i32)
    row_number = iota((64, LANES), 0)
    column_number = iota((256, LANES), 0)
    sums = jnp.zeros((6 * 64, 256), f32)
    batch = 4
    for first in range(0, HULL_DESTS, batch):
        lefts, rights = [], []
        for n in range(batch * HULL_ROWS):
            base = (first + n // HULL_ROWS) * 4 * HULL_ROWS + n % HULL_ROWS
            ids = nodes_ref[base + 3 * HULL_ROWS : base + 3 * HULL_ROWS + 1, :].astype(i32) - 1
            here = row_number == (ids >> 8)
            pieces = []
            for c in range(3):
                values = nodes_ref[base + c * HULL_ROWS : base + c * HULL_ROWS + 1, :]
                pieces.extend(jnp.where(here, part, 0.0).astype(bf16) for part in halves(values))
            lefts.append(jnp.concatenate(pieces, axis=0))
            rights.append(jnp.where(column_number == (ids & 255), 1.0, 0.0).astype(bf16))
        sums = sums + dot_last(jnp.concatenate(lefts, axis=1), jnp.concatenate(rights, axis=1))
    for c in range(3):
        out_ref[c] = sums[2 * c * 64 : (2 * c + 1) * 64] + sums[(2 * c + 1) * 64 : (2 * c + 2) * 64]
    copy = pltpu.make_async_copy(out_ref, out_hbm, sem)
    copy.start()
    copy.wait()


def shaped(*shape, dtype=f32):
    return jax.ShapeDtypeStruct(shape, dtype)


def call(kernel, outs, scratch, cost, *args, places="", out_places=""):
    spaces = {"V": pltpu.VMEM, "S": pltpu.SMEM, "H": pltpu.HBM}

    def specs(count, names):
        names = names + "V" * (count - len(names))
        return [pl.BlockSpec(memory_space=spaces[name]) for name in names]

    args = [pltpu.with_memory_space_constraint(arg, pltpu.HBM) if place == "H" else arg for arg, place in zip(args, places + "V" * len(args))]
    if isinstance(outs, tuple):
        outs = tuple(pltpu.HBM(out.shape, out.dtype) if place == "H" else out for out, place in zip(outs, out_places + "V" * len(outs)))
    return pl.pallas_call(
        kernel,
        out_shape=outs,
        in_specs=specs(len(args), places),
        out_specs=tuple(specs(len(outs), out_places)) if isinstance(outs, tuple) else specs(1, out_places)[0],
        scratch_shapes=scratch,
        compiler_params=PARAMS,
        cost_estimate=pl.CostEstimate(flops=cost, bytes_accessed=1 << 20, transcendentals=0),
        name=getattr(kernel, "func", kernel).__name__,
    )(*args)


def pair_exchange(axis, even, odd):
    count = lax.axis_size(axis)
    results = []
    for first, values in ((0, even), (1, odd)):
        pairs = [(i, (i + 1) % count) for i in range(first, count, 2)]
        results.append(lax.ppermute(values, axis, pairs + [(b, a) for a, b in pairs]))
    return results


def per_device(start_field, stiffness, mass, sens_values, sens_cells, sens_counts, hull_cells, hull_patches):
    slabs = shaped(14, CY, CZ)
    gx, gy, side = (lax.axis_index(axis).astype(i32).reshape(1) for axis in ("gx", "gy", "gz"))
    packed, even, odd = call(
        pack_slots,
        (shaped(3 * BLOCKS, LANES), slabs, slabs),
        [
            pltpu.VMEM((3, SLOT_ROWS, LANES), f32),
            pltpu.VMEM((SLOT_ROWS, LANES), i32),
            pltpu.VMEM((1, BLOCKS), i32),
            pltpu.SemaphoreType.DMA((13,)),
        ],
        1 << 20,
        gx,
        sens_values.reshape(3, SLOT_ROWS, LANES),
        sens_cells.reshape(SLOT_ROWS, LANES),
        sens_counts.reshape(1, BLOCKS),
        start_field,
        stiffness,
        mass,
        places="SHHHHHH",
    )
    packed = packed.reshape(BLOCKS, 1, 3 * LANES)
    arrived = lax.all_to_all(packed, ("gx", "gy"), split_axis=0, concat_axis=0, tiled=True)
    xeven, xodd = pair_exchange("gx", even, odd)
    count = HULL_DESTS * HULL_ROWS
    where, ids = call(
        route_hull,
        (shaped(2 * count, LANES, dtype=i32), shaped(count, LANES)),
        [pltpu.VMEM((4 * count, SLOTS), bf16), pltpu.VMEM((LANES, SLOTS), bf16)],
        1 << 31,
        hull_cells.reshape(SLOT_ROWS, LANES),
        hull_patches.reshape(SLOT_ROWS, LANES),
    )
    arrived = arrived.reshape(3 * BLOCKS, LANES)
    source = call(
        scatter_slots,
        shaped(3, CX + 4, CY, CZ),
        [pltpu.VMEM((rows, SLOTS), bf16) for rows in (2 * LANES, 6 * LANES, 12 * CY, LANES)],
        1 << 32,
        arrived,
    )
    y_message = shaped(CX + 4, Y_ROWS, CZ)
    n_gx, n_gy = lax.axis_size("gx"), lax.axis_size("gy")
    even, odd = call(
        functools.partial(pack_y, n_gx),
        (y_message, y_message),
        [],
        1 << 20,
        gx,
        gy,
        source,
        start_field,
        stiffness,
        mass,
        xeven,
        xodd,
        places="SS",
    )
    yeven, yodd = pair_exchange("gy", even, odd)
    rows = (EXT_X - 2) * EXT_Y
    ext, faces = call(
        functools.partial(widen, n_gx, n_gy),
        (shaped(8, EXT_X, EXT_Y, CZ), shaped(Z_ROWS, rows)),
        [],
        1 << 20,
        gx,
        gy,
        side,
        start_field,
        stiffness,
        mass,
        source,
        xeven,
        xodd,
        yeven,
        yodd,
        places="SSS",
    )
    faces = lax.ppermute(faces, "gz", [(0, 1), (1, 0)])
    wide = (EXT_X - 2, EXT_Y, 2 * CZ)
    full = (EXT_X, EXT_Y, 2 * CZ)
    field, outgoing = call(
        relax_and_gather,
        (shaped(3, CX, CY, CZ), shaped(4 * count, LANES)),
        [
            pltpu.VMEM((3,) + full, f32),
            pltpu.VMEM((3,) + full, f32),
            pltpu.VMEM(full, f32),
            pltpu.VMEM((6,) + wide, f32),
            pltpu.VMEM(wide, f32),
            pltpu.VMEM(wide, f32),
            pltpu.VMEM((3,) + wide, f32),
            pltpu.VMEM((3 * LANES, 4 * LANES), bf16),
        ],
        1 << 32,
        side,
        ext,
        faces,
        where,
        ids,
        places="S",
    )
    outgoing = outgoing.reshape(HULL_DESTS, 1, 4 * HULL_ROWS * LANES)
    nodes = lax.all_to_all(outgoing, ("gy", "gz"), split_axis=0, concat_axis=0, tiled=True)
    nodes = nodes.reshape(4 * count, LANES)
    patch, overflow = call(
        scatter_hull,
        (shaped(3, 64, 256), shaped(1, dtype=i32)),
        [pltpu.VMEM((3, 64, 256), f32), pltpu.SemaphoreType.DMA],
        1 << 32,
        nodes,
        out_places="HS",
    )

    def in_messages():
        return patch

    def every_node():
        cells = hull_cells[0, 0]
        values = field.reshape(3, -1)[:, cells] * stiffness.reshape(-1)[cells]
        sent = jnp.concatenate([values, hull_patches[0].astype(f32)], axis=0)
        sent = jnp.broadcast_to(sent[None], (HULL_DESTS,) + sent.shape)
        got = lax.all_to_all(sent, ("gy", "gz"), split_axis=0, concat_axis=0, tiled=True)
        got = jnp.swapaxes(got, 0, 1).reshape(4, -1)
        spots = got[3].astype(i32) - lax.axis_index(("gy", "gz")) * PATCH_BLOCK
        mine = (spots >= 0) & (spots < PATCH_BLOCK)
        added = jnp.where(mine, got[:3], 0.0)
        patch = jnp.zeros((3, PATCH_BLOCK), f32).at[:, jnp.where(mine, spots, 0)].add(added)
        return patch.reshape(3, 64, 256)

    patch = lax.cond(overflow[0] > 0, every_node, in_messages)
    return field, patch


def solution(mesh):
    placed = (
        P(None, "gx", "gy", "gz"),
        P("gx", "gy", "gz"),
        P("gx", "gy", "gz"),
        P(None, "gz", ("gx", "gy"), None),
        P("gz", ("gx", "gy"), None),
        P("gz", ("gx", "gy"), None),
        P("gx", ("gy", "gz"), None),
        P("gx", ("gy", "gz"), None),
    )
    return jax.shard_map(
        per_device,
        mesh=mesh,
        in_specs=placed,
        out_specs=(P(None, "gx", "gy", "gz"), P(None, ("gy", "gz"), "gx")),
        check_vma=False,
    )
```

```python
import functools

import jax
import jax.numpy as jnp
from jax import lax
from jax.experimental import pallas as pl
from jax.experimental.pallas import tpu as pltpu
from jax.sharding import PartitionSpec as P

CX, CY, CZ = 8, 24, 128
LANES = 128
SLOTS = 4096
SLOT_ROWS = SLOTS // LANES
BLOCKS = 128
CAP = 32
HULL_DESTS = 16
PATCH_BLOCK = 64 * 256
HULL_ROWS = 3
HULL_CAP = HULL_ROWS * LANES - 1
Y_ROWS = 14
Y_FIELDS = ((0, 3), (3, 3), (6, 3), (9, 3), (12, 2))
Z_ROWS = 16
EXT_X = CX + 6
EXT_Y = 32
RELAX = 0.8

f32, bf16, i32 = jnp.float32, jnp.bfloat16, jnp.int32
PARAMS = pltpu.CompilerParams(vmem_limit_bytes=24 * 1024 * 1024)


def iota(shape, dim):
    return lax.broadcasted_iota(i32, shape, dim)


def halves(values):
    high = values.astype(bf16).astype(f32)
    return high, values - high


def dot_last(a, b):
    return lax.dot_general(a, b, (((1,), (1,)), ((), ())), preferred_element_type=f32)


def by_parity(place, even, odd):
    index, count = place
    is_odd = lax.rem(index, 2) == 1
    low = jnp.where(is_odd, even, odd) * jnp.where(index > 0, 1.0, 0.0)
    high = jnp.where(is_odd, odd, even) * jnp.where(index < count - 1, 1.0, 0.0)
    return low, high


def pack_slots(
    gx_ref, values_hbm, cells_hbm, counts_hbm, field_hbm, stiff_hbm, mass_hbm, out_ref, even_ref, odd_ref, values_ref, cells_ref, counts_ref, sems
):
    copies = [
        pltpu.make_async_copy(values_hbm, values_ref, sems.at[0]),
        pltpu.make_async_copy(cells_hbm, cells_ref, sems.at[1]),
        pltpu.make_async_copy(counts_hbm, counts_ref, sems.at[2]),
    ]
    odd = lax.rem(gx_ref[0], 2)
    for slab, up in ((even_ref, 1 - odd), (odd_ref, odd)):
        planes, mass_planes = pl.ds(up * (CX - 3), 3), pl.ds(up * (CX - 2), 2)
        for c in range(3):
            copies.append(pltpu.make_async_copy(field_hbm.at[c, planes], slab.at[pl.ds(3 * c, 3)], sems.at[len(copies)]))
        copies.append(pltpu.make_async_copy(stiff_hbm.at[planes], slab.at[pl.ds(9, 3)], sems.at[len(copies)]))
        copies.append(pltpu.make_async_copy(mass_hbm.at[mass_planes], slab.at[pl.ds(12, 2)], sems.at[len(copies)]))
    for copy in copies:
        copy.start()
    for copy in copies[:3]:
        copy.wait()
    counts = counts_ref[...].astype(f32)
    spread = jnp.where(iota((SLOT_ROWS, BLOCKS), 1) // 4 == iota((SLOT_ROWS, BLOCKS), 0), counts, 0.0)
    place = jnp.where(iota((BLOCKS, LANES), 0) % 4 == iota((BLOCKS, LANES), 1) // CAP, 1.0, 0.0)
    limits = jnp.dot(spread.astype(bf16), place.astype(bf16), preferred_element_type=f32)
    lane = iota((SLOT_ROWS, LANES), 1)
    live = (lane % CAP).astype(f32) < limits
    parts = [jnp.where(live, values_ref[c], 0.0) for c in range(3)] + [cells_ref[...].astype(f32)]
    quarter = lane // CAP
    row = iota((SLOT_ROWS, LANES), 0)
    for q in range(4):
        message = jnp.zeros((SLOT_ROWS, LANES), f32)
        for c in range(4):
            turned = parts[c] if c == q else pltpu.roll(parts[c], (c - q) * CAP % LANES, 1)
            message = jnp.where(quarter == c, turned, message)
        below = jnp.where(row >= 2, pltpu.roll(message, 2, 0), 0.0)
        above = jnp.where(row < SLOT_ROWS - 2, pltpu.roll(message, SLOT_ROWS - 2, 0), 0.0)
        out_ref[pl.ds(3 * q, SLOT_ROWS, stride=12), :] = below
        out_ref[pl.ds(3 * q + 1, SLOT_ROWS, stride=12), :] = message
        out_ref[pl.ds(3 * q + 2, SLOT_ROWS, stride=12), :] = above
    for copy in copies[3:]:
        copy.wait()


def scatter_slots(gy_ref, slots_ref, source_ref, even_ref, odd_ref, rows_s, lanes_s, left_s, right_s):
    lane = iota((SLOT_ROWS, LANES), 1)
    quarter = lane // CAP
    own_rows = CY * CX
    side_rows = CY * 2

    def unpack(k):
        parts = [jnp.zeros((SLOT_ROWS, LANES), f32) for _ in range(4)]
        for q in range(4):
            message = slots_ref[pl.ds(3 * q + k, SLOT_ROWS, stride=12), :]
            for c in range(4):
                turned = message if c == q else pltpu.roll(message, (q - c) * CAP % LANES, 1)
                parts[c] = jnp.where(quarter == q, turned, parts[c])
        ids = parts[3].astype(i32)
        pieces = []
        for c in range(3):
            pieces.extend(halves(parts[c]))
        return ids // LANES, ids % LANES, pieces

    lane_number = iota((LANES, LANES), 0)
    row_number = iota((2 * LANES, LANES), 0)
    side_number = iota((side_rows, LANES), 0)
    rows, lanes, pieces = unpack(1)
    for r in range(SLOT_ROWS):
        cut = slice(r * LANES, (r + 1) * LANES)
        rows_s[:, cut] = jnp.where(row_number == rows[r : r + 1, :], 1.0, 0.0).astype(bf16)
        here = lane_number == lanes[r : r + 1, :]
        for n in range(6):
            lanes_s[n * LANES : (n + 1) * LANES, cut] = jnp.where(here, pieces[n][r : r + 1, :], 0.0).astype(bf16)
    sums = dot_last(lanes_s[...], rows_s[...])
    for c in range(3):
        one = sums[2 * c * LANES : (2 * c + 1) * LANES] + sums[(2 * c + 1) * LANES : (2 * c + 2) * LANES]
        source_ref[c, 2 : 2 + CX] = jnp.transpose(one)[:own_rows].reshape(CX, CY, LANES)
    for k, first, target in ((0, own_rows - side_rows, 0), (2, 0, 2 + CX)):
        rows, lanes, pieces = unpack(k)
        for r in range(SLOT_ROWS):
            cut = slice(r * LANES, (r + 1) * LANES)
            here = side_number == rows[r : r + 1, :] - first
            for n in range(6):
                left_s[n * side_rows : (n + 1) * side_rows, cut] = jnp.where(here, pieces[n][r : r + 1, :], 0.0).astype(bf16)
            right_s[:, cut] = jnp.where(lane_number == lanes[r : r + 1, :], 1.0, 0.0).astype(bf16)
        sums = dot_last(left_s[...], right_s[...])
        for c in range(3):
            one = sums[2 * c * side_rows : (2 * c + 1) * side_rows] + sums[(2 * c + 1) * side_rows : (2 * c + 2) * side_rows]
            source_ref[c, target : target + 2] = one.reshape(2, CY, LANES)
    is_odd = lax.rem(gy_ref[0], 2) == 1
    for c in range(3):
        here = slice(2 * c, 2 * c + 2)
        first, last = source_ref[c, :, 0:2, :], source_ref[c, :, CY - 2 :, :]
        even_ref[:, here, :] = jnp.where(is_odd, first, last)
        odd_ref[:, here, :] = jnp.where(is_odd, last, first)


def pack_y(n_gx, gx_ref, gy_ref, field_hbm, stiff_hbm, mass_hbm, xeven_ref, xodd_ref, even_ref, odd_ref, ends_ref, sems):
    copies = []
    for number in range(5):
        own = field_hbm.at[number] if number < 3 else (stiff_hbm if number == 3 else mass_hbm)
        for n, rows in enumerate((pl.ds(0, 8), pl.ds(CY - 8, 8))):
            copies.append(pltpu.make_async_copy(own.at[:, rows], ends_ref.at[number, n], sems.at[len(copies)]))
    for copy in copies:
        copy.start()
    for copy in copies:
        copy.wait()
    is_odd = lax.rem(gy_ref[0], 2) == 1
    for number, (start, width) in enumerate(Y_FIELDS):
        here = slice(start, start + width)
        planes = slice(3 * number, 3 * number + 3) if number < 4 else slice(12, 14)
        pieces = [[], []]
        for n, (rows, own_rows) in enumerate(((slice(0, width), slice(0, width)), (slice(CY - width, CY), slice(8 - width, 8)))):
            low, high = by_parity((gx_ref[0], n_gx), xeven_ref[planes, rows, :], xodd_ref[planes, rows, :])
            own = ends_ref[number, n, :, own_rows, :]
            pieces[n].extend([(slice(0, 2), low[-2:]), (slice(2, 2 + CX), own), (slice(2 + CX, CX + 4), high[:2])])
        for (where, first), (_, last) in zip(*pieces):
            even_ref[where, here, :] = jnp.where(is_odd, first, last)
            odd_ref[where, here, :] = jnp.where(is_odd, last, first)


def route_hull(cells_ref, patches_ref, where_ref, ids_ref, rows_s, lanes_s):
    patches = patches_ref[...]
    cells = cells_ref[...]
    dest = patches // PATCH_BLOCK
    local = patches % PATCH_BLOCK
    hits = [jnp.where(dest == d, 1.0, 0.0) for d in range(HULL_DESTS)]
    stacked = jnp.concatenate(hits, axis=0).astype(bf16)
    upto = jnp.where(iota((LANES, LANES), 0) <= iota((LANES, LANES), 1), 1.0, 0.0).astype(bf16)
    total = HULL_DESTS * SLOT_ROWS
    within = jnp.dot(stacked, upto, preferred_element_type=f32)
    row_sums = jnp.dot(stacked, jnp.ones((LANES, LANES), bf16), preferred_element_type=f32)
    a, b = iota((total, total), 0), iota((total, total), 1)
    earlier = jnp.where((a // SLOT_ROWS == b // SLOT_ROWS) & (b < a), 1.0, 0.0).astype(bf16)
    offsets = jnp.dot(earlier, row_sums.astype(bf16), preferred_element_type=f32)
    rank = jnp.zeros((SLOT_ROWS, LANES), f32)
    for d in range(HULL_DESTS):
        cut = slice(d * SLOT_ROWS, (d + 1) * SLOT_ROWS)
        rank = rank + hits[d] * (within[cut] + offsets[cut] - 1.0)
    rank = rank.astype(i32)
    overflow = jnp.max(jnp.where(rank >= HULL_CAP, 1.0, 0.0))
    slot_row = jnp.where(rank < HULL_CAP, dest * HULL_ROWS + rank // LANES, -1)
    slot_lane = rank % LANES
    payload = [cells // LANES, cells % LANES, local // 256 + 1, local % 256]
    payload = [p.astype(f32) for p in payload]
    count = HULL_DESTS * HULL_ROWS
    row_number = iota((count, LANES), 0)
    lane_number = iota((LANES, LANES), 0)
    for r in range(SLOT_ROWS):
        cut = slice(r * LANES, (r + 1) * LANES)
        here = row_number == slot_row[r : r + 1, :]
        for n in range(4):
            rows_s[n * count : (n + 1) * count, cut] = jnp.where(here, payload[n][r : r + 1, :], 0.0).astype(bf16)
        lanes_s[:, cut] = jnp.where(lane_number == slot_lane[r : r + 1, :], 1.0, 0.0).astype(bf16)
    placed = dot_last(rows_s[...], lanes_s[...])
    where_ref[...] = placed[: 2 * count].astype(i32)
    ids = jnp.maximum((placed[2 * count : 3 * count] - 1.0) * 256.0 + placed[3 * count :] + 1.0, 0.0)
    last = (iota((count, LANES), 1) == LANES - 1) & (row_number % HULL_ROWS == HULL_ROWS - 1)
    ids_ref[...] = jnp.where(last, overflow, ids)


def pack_z(side, arrays, z_ref):
    lane = iota((1, 1, LANES), 2)
    total = jnp.zeros((EXT_X - 2, EXT_Y, LANES), f32)
    for number, array in enumerate(arrays):
        shift = jnp.where(side == 0, (3 * number + 3) % LANES, 3 * number)
        turned = pltpu.roll(array.reshape((EXT_X - 2) * EXT_Y, LANES), shift, 1).reshape(EXT_X - 2, EXT_Y, LANES)
        total = jnp.where((lane >= 3 * number) & (lane < 3 * number + 3), turned, total)
    z_ref[...] = jnp.transpose(total.reshape((EXT_X - 2) * EXT_Y, LANES))[:Z_ROWS]


def unpack_z(side, z_ref):
    rows = (EXT_X - 2) * EXT_Y
    lane = iota((1, 1, LANES), 2)
    columns = jnp.transpose(jnp.concatenate([z_ref[...], jnp.zeros((LANES - Z_ROWS, rows), f32)], axis=0))
    first_lane = jnp.where(side == 0, 0, LANES - 3)
    near = (lane >= first_lane) & (lane < first_lane + 3)

    def beyond(number):
        shift = jnp.where(side == 0, (LANES - 3 * number) % LANES, (2 * LANES - 3 - 3 * number) % LANES)
        return jnp.where(near, pltpu.roll(columns, shift, 1).reshape(EXT_X - 2, EXT_Y, LANES), 0.0)

    return beyond


def widen_fixed(n_gx, n_gy, gx_ref, gy_ref, side_ref, field_ref, stiff_ref, mass_ref, xeven_ref, xodd_ref, yeven_ref, yodd_ref, ext_ref, z_ref):
    zeros = jnp.zeros((EXT_X, EXT_Y - CY, LANES), f32)
    for number, (start, width) in enumerate(Y_FIELDS):
        target = ext_ref.at[number]
        target[:, CY:, :] = zeros
        planes = slice(3 * number, 3 * number + 3) if number < 4 else slice(12, 14)
        low, high = by_parity((gx_ref[0], n_gx), xeven_ref[planes], xodd_ref[planes])
        own = field_ref.at[number] if number < 3 else (stiff_ref if number == 3 else mass_ref)
        if width < 3:
            target[0, :CY, :] = jnp.zeros((CY, LANES), f32)
            target[EXT_X - 1, :CY, :] = jnp.zeros((CY, LANES), f32)
        target[3 - width : 3, :CY, :] = low
        target[3 : 3 + CX, :CY, :] = own[...]
        target[3 + CX : 3 + CX + width, :CY, :] = high
        here = slice(start, start + width)
        low, high = by_parity((gy_ref[0], n_gy), yeven_ref[:, here, :], yodd_ref[:, here, :])
        target[1 : EXT_X - 1, CY : CY + width, :] = high
        target[1 : EXT_X - 1, EXT_Y - width :, :] = low
    pack_z(side_ref[0], [ext_ref[number, 1 : EXT_X - 1] for number in range(5)], z_ref)


def widen_source(n_gy, gy_ref, side_ref, source_ref, yeven_ref, yodd_ref, ext_ref, z_ref):
    zeros = jnp.zeros((EXT_X - 2, EXT_Y - CY, LANES), f32)
    for c in range(3):
        here = slice(2 * c, 2 * c + 2)
        low, high = by_parity((gy_ref[0], n_gy), yeven_ref[:, here, :], yodd_ref[:, here, :])
        ext_ref[c, :, CY:, :] = zeros
        ext_ref[c, :, :CY, :] = source_ref[c]
        ext_ref[c, :, CY : CY + 2, :] = high
        ext_ref[c, :, EXT_Y - 2 :, :] = low
    pack_z(side_ref[0], [ext_ref[c] for c in range(3)], z_ref)


def around(ref_at, x):
    middle = ref_at(x)
    return middle, (
        ref_at(x + 1),
        ref_at(x - 1),
        pltpu.roll(middle, EXT_Y - 1, 0),
        pltpu.roll(middle, 1, 0),
        pltpu.roll(middle, 2 * LANES - 1, 1),
        pltpu.roll(middle, 1, 1),
    )


def prepare(side_ref, ext_ref, z_ref, start_ref, weight_ref, keep_ref, couple_ref, rate_ref, stiff_s, mass_s):
    beyond = unpack_z(side_ref[0], z_ref)
    empty = jnp.zeros((EXT_Y, LANES), f32)
    for c in range(3):
        start_ref[c, :, :, :LANES] = ext_ref[c]
        start_ref[c, 1 : EXT_X - 1, :, LANES:] = beyond(c)
        start_ref[c, 0, :, LANES:] = empty
        start_ref[c, EXT_X - 1, :, LANES:] = empty
    stiff_s[:, :, :LANES] = ext_ref[3]
    stiff_s[1 : EXT_X - 1, :, LANES:] = beyond(3)
    stiff_s[0, :, LANES:] = empty
    stiff_s[EXT_X - 1, :, LANES:] = empty
    mass_s[:, :, :LANES] = ext_ref[4, 1 : EXT_X - 1]
    mass_s[:, :, LANES:] = beyond(4)

    def one(i, carry):
        middle, others = around(lambda x: stiff_s[x], i + 1)
        weights = [0.5 * (middle + other) for other in others]
        weight_sum = weights[0] + weights[1] + weights[2] + weights[3] + weights[4] + weights[5]
        mass = mass_s[i]
        inside = middle > 0.0
        rate = jnp.where(inside, RELAX / jnp.where(inside, weight_sum + 1.25 * mass, 1.0), 0.0)
        for n in range(6):
            weight_ref[n, i] = rate * weights[n]
        keep_ref[i] = jnp.where(inside, 1.0 - rate * (weight_sum + mass), 0.0)
        couple_ref[i] = 0.25 * rate * mass
        rate_ref[i] = rate
        return carry

    lax.fori_loop(0, EXT_X - 2, one, 0)


def relax_and_gather(
    side_ref,
    start_ref,
    weight_s,
    keep_s,
    couple_s,
    rate_ref,
    ext_ref,
    z_ref,
    stiff_ref,
    where_ref,
    ids_ref,
    out_ref,
    message_ref,
    first_s,
    second_s,
    push_s,
    turned_s,
):
    beyond = unpack_z(side_ref[0], z_ref)
    for c in range(3):
        push_s[c, :, :, :LANES] = rate_ref[:, :, :LANES] * ext_ref[c]
        push_s[c, :, :, LANES:] = rate_ref[:, :, LANES:] * beyond(c)

    def sweep(source, target, lowest, highest):
        def one(x, carry):
            i = x - 1
            gathered = [around(lambda y, c=c: source[c, y], x) for c in range(3)]
            shared = couple_s[i] * (gathered[0][0] + gathered[1][0] + gathered[2][0])
            for c in range(3):
                middle, others = gathered[c]
                value = keep_s[i] * middle + (push_s[c, i] - shared)
                for n in range(6):
                    value = value + weight_s[n, i] * others[n]
                target[c, x] = value
            return carry

        lax.fori_loop(lowest, highest, one, 0)

    sweep(start_ref, second_s, 1, EXT_X - 1)
    sweep(second_s, first_s, 2, EXT_X - 2)

    def finish(x, carry):
        i = x - 1
        middles = [first_s[c, x, :CY, :LANES] for c in range(3)]
        shared = couple_s[i, :CY, :LANES] * (middles[0] + middles[1] + middles[2])
        for c in range(3):
            columns = first_s[c, x, :, :LANES]
            halo = first_s[c, x, :CY, LANES:]
            others = (
                first_s[c, x + 1, :CY, :LANES],
                first_s[c, x - 1, :CY, :LANES],
                pltpu.roll(columns, EXT_Y - 1, 0)[:CY],
                pltpu.roll(columns, 1, 0)[:CY],
                pltpu.roll(jnp.where(last_lane == 0, halo, middles[c]), LANES - 1, 1),
                pltpu.roll(jnp.where(last_lane == LANES - 1, halo, middles[c]), 1, 1),
            )
            value = keep_s[i, :CY, :LANES] * middles[c] + (push_s[c, i, :CY, :LANES] - shared)
            for n in range(6):
                value = value + weight_s[n, i, :CY, :LANES] * others[n]
            out_ref[c, x - 3] = value
        return carry

    last_lane = iota((CY, LANES), 1)
    lax.fori_loop(3, 3 + CX, finish, 0)

    own_rows = CX * CY
    blank = jnp.zeros((2 * LANES - own_rows, LANES), f32)
    for c in range(3):
        result = out_ref[c]
        scaled = (result * stiff_ref[...]).reshape(own_rows, LANES)
        high, low = halves(scaled)
        cut = slice(c * LANES, (c + 1) * LANES)
        turned_s[cut, : 2 * LANES] = jnp.transpose(jnp.concatenate([high, blank], axis=0)).astype(bf16)
        turned_s[cut, 2 * LANES :] = jnp.transpose(jnp.concatenate([low, blank], axis=0)).astype(bf16)
    count = HULL_DESTS * HULL_ROWS
    row_number = iota((2 * LANES, LANES), 0)
    lane_number = iota((LANES, LANES), 0)
    group = 2 * HULL_ROWS
    for g in range(count // group):
        chosen = []
        for i in range(group):
            r = g * group + i
            chosen.append(jnp.where(row_number == where_ref[r : r + 1, :], 1.0, 0.0).astype(bf16))
        chosen = jnp.concatenate(chosen, axis=1)
        found = jnp.dot(turned_s[...], jnp.concatenate([chosen, chosen], axis=0), preferred_element_type=f32)
        for i in range(group):
            r = g * group + i
            here = lane_number == where_ref[count + r : count + r + 1, :]
            base = r // HULL_ROWS * 4 * HULL_ROWS + r % HULL_ROWS
            for c in range(3):
                part = found[c * LANES : (c + 1) * LANES, i * LANES : (i + 1) * LANES]
                spot = base + c * HULL_ROWS
                message_ref[spot : spot + 1, :] = jnp.sum(jnp.where(here, part, 0.0), axis=0, keepdims=True)
            spot = base + 3 * HULL_ROWS
            message_ref[spot : spot + 1, :] = ids_ref[r : r + 1, :]


def scatter_hull(nodes_ref, out_hbm, overflow_ref, out_ref, sem):
    flags = nodes_ref[pl.ds(4 * HULL_ROWS - 1, HULL_DESTS, stride=4 * HULL_ROWS), :]
    last = iota((HULL_DESTS, LANES), 1) == LANES - 1
    overflow_ref[0] = jnp.max(jnp.where(last, flags, 0.0)).astype(i32)
    row_number = iota((64, LANES), 0)
    column_number = iota((256, LANES), 0)
    sums = jnp.zeros((6 * 64, 256), f32)
    batch = 4
    for first in range(0, HULL_DESTS, batch):
        lefts, rights = [], []
        for n in range(batch * HULL_ROWS):
            base = (first + n // HULL_ROWS) * 4 * HULL_ROWS + n % HULL_ROWS
            ids = nodes_ref[base + 3 * HULL_ROWS : base + 3 * HULL_ROWS + 1, :].astype(i32) - 1
            here = row_number == (ids >> 8)
            pieces = []
            for c in range(3):
                values = nodes_ref[base + c * HULL_ROWS : base + c * HULL_ROWS + 1, :]
                pieces.extend(jnp.where(here, part, 0.0).astype(bf16) for part in halves(values))
            lefts.append(jnp.concatenate(pieces, axis=0))
            rights.append(jnp.where(column_number == (ids & 255), 1.0, 0.0).astype(bf16))
        sums = sums + dot_last(jnp.concatenate(lefts, axis=1), jnp.concatenate(rights, axis=1))
    for c in range(3):
        out_ref[c] = sums[2 * c * 64 : (2 * c + 1) * 64] + sums[(2 * c + 1) * 64 : (2 * c + 2) * 64]
    copy = pltpu.make_async_copy(out_ref, out_hbm, sem)
    copy.start()
    copy.wait()


def shaped(*shape, dtype=f32):
    return jax.ShapeDtypeStruct(shape, dtype)


def call(kernel, outs, scratch, cost, *args, places="", out_places=""):
    spaces = {"V": pltpu.VMEM, "S": pltpu.SMEM, "H": pltpu.HBM}

    def specs(count, names):
        names = names + "V" * (count - len(names))
        return [pl.BlockSpec(memory_space=spaces[name]) for name in names]

    args = [pltpu.with_memory_space_constraint(arg, pltpu.HBM) if place == "H" else arg for arg, place in zip(args, places + "V" * len(args))]
    if isinstance(outs, tuple):
        outs = tuple(pltpu.HBM(out.shape, out.dtype) if place == "H" else out for out, place in zip(outs, out_places + "V" * len(outs)))
    return pl.pallas_call(
        kernel,
        out_shape=outs,
        in_specs=specs(len(args), places),
        out_specs=tuple(specs(len(outs), out_places)) if isinstance(outs, tuple) else specs(1, out_places)[0],
        scratch_shapes=scratch,
        compiler_params=PARAMS,
        cost_estimate=pl.CostEstimate(flops=cost, bytes_accessed=1 << 20, transcendentals=0),
        name=getattr(kernel, "func", kernel).__name__,
    )(*args)


def pair_exchange(axis, even, odd):
    count = lax.axis_size(axis)
    results = []
    for first, values in ((0, even), (1, odd)):
        pairs = [(i, (i + 1) % count) for i in range(first, count, 2)]
        results.append(lax.ppermute(values, axis, pairs + [(b, a) for a, b in pairs]))
    return results


def per_device(start_field, stiffness, mass, sens_values, sens_cells, sens_counts, hull_cells, hull_patches):
    slabs = shaped(14, CY, CZ)
    gx, gy, side = (lax.axis_index(axis).astype(i32).reshape(1) for axis in ("gx", "gy", "gz"))
    packed, even, odd = call(
        pack_slots,
        (shaped(3 * BLOCKS, LANES), slabs, slabs),
        [
            pltpu.VMEM((3, SLOT_ROWS, LANES), f32),
            pltpu.VMEM((SLOT_ROWS, LANES), i32),
            pltpu.VMEM((1, BLOCKS), i32),
            pltpu.SemaphoreType.DMA((13,)),
        ],
        1 << 20,
        gx,
        sens_values.reshape(3, SLOT_ROWS, LANES),
        sens_cells.reshape(SLOT_ROWS, LANES),
        sens_counts.reshape(1, BLOCKS),
        start_field,
        stiffness,
        mass,
        places="SHHHHHH",
    )
    packed = packed.reshape(BLOCKS, 1, 3 * LANES)
    arrived = lax.all_to_all(packed, ("gx", "gy"), split_axis=0, concat_axis=0, tiled=True)
    xeven, xodd = pair_exchange("gx", even, odd)
    count = HULL_DESTS * HULL_ROWS
    where, ids = call(
        route_hull,
        (shaped(2 * count, LANES, dtype=i32), shaped(count, LANES)),
        [pltpu.VMEM((4 * count, SLOTS), bf16), pltpu.VMEM((LANES, SLOTS), bf16)],
        1 << 31,
        hull_cells.reshape(SLOT_ROWS, LANES),
        hull_patches.reshape(SLOT_ROWS, LANES),
    )
    n_gx, n_gy = lax.axis_size("gx"), lax.axis_size("gy")
    y_message = shaped(CX + 4, Y_ROWS, CZ)
    even, odd = call(
        functools.partial(pack_y, n_gx),
        (y_message, y_message),
        [pltpu.VMEM((5, 2, CX, 8, CZ), f32), pltpu.SemaphoreType.DMA((10,))],
        1 << 34,
        gx,
        gy,
        start_field,
        stiffness,
        mass,
        xeven,
        xodd,
        places="SSHHH",
    )
    yeven, yodd = pair_exchange("gy", even, odd)
    arrived, yeven, yodd = lax.optimization_barrier((arrived, yeven, yodd))
    y_message = shaped(CX + 4, 6, CZ)
    source, even, odd = call(
        scatter_slots,
        (shaped(3, CX + 4, CY, CZ), y_message, y_message),
        [pltpu.VMEM((rows, SLOTS), bf16) for rows in (2 * LANES, 6 * LANES, 12 * CY, LANES)],
        1 << 32,
        gy,
        arrived.reshape(3 * BLOCKS, LANES),
        places="S",
    )
    rows = (EXT_X - 2) * EXT_Y
    z_message = shaped(Z_ROWS, rows)
    source_even, source_odd = pair_exchange("gy", even, odd)
    ext, faces = call(
        functools.partial(widen_fixed, n_gx, n_gy),
        (shaped(5, EXT_X, EXT_Y, CZ), z_message),
        [],
        1 << 20,
        gx,
        gy,
        side,
        start_field,
        stiffness,
        mass,
        xeven,
        xodd,
        yeven,
        yodd,
        places="SSS",
    )
    faces = lax.ppermute(faces, "gz", [(0, 1), (1, 0)])
    source_ext, source_faces = call(
        functools.partial(widen_source, n_gy),
        (shaped(3, EXT_X - 2, EXT_Y, CZ), z_message),
        [],
        1 << 20,
        gy,
        side,
        source,
        source_even,
        source_odd,
        places="SS",
    )
    source_faces = lax.ppermute(source_faces, "gz", [(0, 1), (1, 0)])
    wide = (EXT_X - 2, EXT_Y, 2 * CZ)
    full = (EXT_X, EXT_Y, 2 * CZ)
    prepared = call(
        prepare,
        (shaped(3, *full), shaped(6, *wide), shaped(*wide), shaped(*wide), shaped(*wide)),
        [pltpu.VMEM(full, f32), pltpu.VMEM(wide, f32)],
        1 << 30,
        side,
        ext,
        faces,
        places="S",
    )
    field, outgoing = call(
        relax_and_gather,
        (shaped(3, CX, CY, CZ), shaped(4 * count, LANES)),
        [
            pltpu.VMEM((3,) + full, f32),
            pltpu.VMEM((3,) + full, f32),
            pltpu.VMEM((3,) + wide, f32),
            pltpu.VMEM((3 * LANES, 4 * LANES), bf16),
        ],
        1 << 32,
        side,
        *prepared,
        source_ext,
        source_faces,
        stiffness,
        where,
        ids,
        places="S",
    )
    outgoing = outgoing.reshape(HULL_DESTS, 1, 4 * HULL_ROWS * LANES)
    nodes = lax.all_to_all(outgoing, ("gy", "gz"), split_axis=0, concat_axis=0, tiled=True)
    nodes = nodes.reshape(4 * count, LANES)
    patch, overflow = call(
        scatter_hull,
        (shaped(3, 64, 256), shaped(1, dtype=i32)),
        [pltpu.VMEM((3, 64, 256), f32), pltpu.SemaphoreType.DMA],
        1 << 32,
        nodes,
        out_places="HS",
    )

    def in_messages():
        return patch

    def every_node():
        cells = hull_cells[0, 0]
        values = field.reshape(3, -1)[:, cells] * stiffness.reshape(-1)[cells]
        sent = jnp.concatenate([values, hull_patches[0].astype(f32)], axis=0)
        sent = jnp.broadcast_to(sent[None], (HULL_DESTS,) + sent.shape)
        got = lax.all_to_all(sent, ("gy", "gz"), split_axis=0, concat_axis=0, tiled=True)
        got = jnp.swapaxes(got, 0, 1).reshape(4, -1)
        spots = got[3].astype(i32) - lax.axis_index(("gy", "gz")) * PATCH_BLOCK
        mine = (spots >= 0) & (spots < PATCH_BLOCK)
        added = jnp.where(mine, got[:3], 0.0)
        patch = jnp.zeros((3, PATCH_BLOCK), f32).at[:, jnp.where(mine, spots, 0)].add(added)
        return patch.reshape(3, 64, 256)

    patch = lax.cond(overflow[0] > 0, every_node, in_messages)
    return field, patch


def solution(mesh):
    placed = (
        P(None, "gx", "gy", "gz"),
        P("gx", "gy", "gz"),
        P("gx", "gy", "gz"),
        P(None, "gz", ("gx", "gy"), None),
        P("gz", ("gx", "gy"), None),
        P("gz", ("gx", "gy"), None),
        P("gx", ("gy", "gz"), None),
        P("gx", ("gy", "gz"), None),
    )
    return jax.shard_map(
        per_device,
        mesh=mesh,
        in_specs=placed,
        out_specs=(P(None, "gx", "gy", "gz"), P(None, ("gy", "gz"), "gx")),
        check_vma=False,
    )
```

```python
import functools

import jax
import jax.numpy as jnp
from jax import lax
from jax.experimental import pallas as pl
from jax.experimental.pallas import tpu as pltpu
from jax.sharding import PartitionSpec as P

CX, CY, CZ = 8, 24, 128
LANES = 128
SLOTS = 4096
SLOT_ROWS = SLOTS // LANES
BLOCKS = 128
CAP = 32
HULL_DESTS = 16
PATCH_BLOCK = 64 * 256
HULL_ROWS = 3
HULL_CAP = HULL_ROWS * LANES - 1
Y_ROWS = 14
Y_FIELDS = ((0, 3), (3, 3), (6, 3), (9, 3), (12, 2))
Z_ROWS = 16
EXT_X = CX + 6
EXT_Y = 32
RELAX = 0.8

f32, bf16, i32 = jnp.float32, jnp.bfloat16, jnp.int32
PARAMS = pltpu.CompilerParams(vmem_limit_bytes=24 * 1024 * 1024)


def iota(shape, dim):
    return lax.broadcasted_iota(i32, shape, dim)


def halves(values):
    high = values.astype(bf16).astype(f32)
    return high, values - high


def dot_last(a, b):
    return lax.dot_general(a, b, (((1,), (1,)), ((), ())), preferred_element_type=f32)


def by_parity(place, even, odd):
    index, count = place
    is_odd = lax.rem(index, 2) == 1
    low = jnp.where(is_odd, even, odd) * jnp.where(index > 0, 1.0, 0.0)
    high = jnp.where(is_odd, odd, even) * jnp.where(index < count - 1, 1.0, 0.0)
    return low, high


def pack_slots(
    gx_ref, values_hbm, cells_hbm, counts_hbm, field_hbm, stiff_hbm, mass_hbm, out_ref, even_ref, odd_ref, values_ref, cells_ref, counts_ref, sems
):
    copies = [
        pltpu.make_async_copy(values_hbm, values_ref, sems.at[0]),
        pltpu.make_async_copy(cells_hbm, cells_ref, sems.at[1]),
        pltpu.make_async_copy(counts_hbm, counts_ref, sems.at[2]),
    ]
    odd = lax.rem(gx_ref[0], 2)
    for slab, up in ((even_ref, 1 - odd), (odd_ref, odd)):
        planes, mass_planes = pl.ds(up * (CX - 3), 3), pl.ds(up * (CX - 2), 2)
        for c in range(3):
            copies.append(pltpu.make_async_copy(field_hbm.at[c, planes], slab.at[pl.ds(3 * c, 3)], sems.at[len(copies)]))
        copies.append(pltpu.make_async_copy(stiff_hbm.at[planes], slab.at[pl.ds(9, 3)], sems.at[len(copies)]))
        copies.append(pltpu.make_async_copy(mass_hbm.at[mass_planes], slab.at[pl.ds(12, 2)], sems.at[len(copies)]))
    for copy in copies:
        copy.start()
    for copy in copies[:3]:
        copy.wait()
    counts = counts_ref[...].astype(f32)
    spread = jnp.where(iota((SLOT_ROWS, BLOCKS), 1) // 4 == iota((SLOT_ROWS, BLOCKS), 0), counts, 0.0)
    place = jnp.where(iota((BLOCKS, LANES), 0) % 4 == iota((BLOCKS, LANES), 1) // CAP, 1.0, 0.0)
    limits = jnp.dot(spread.astype(bf16), place.astype(bf16), preferred_element_type=f32)
    lane = iota((SLOT_ROWS, LANES), 1)
    live = (lane % CAP).astype(f32) < limits
    parts = [jnp.where(live, values_ref[c], 0.0) for c in range(3)] + [cells_ref[...].astype(f32)]
    quarter = lane // CAP
    row = iota((SLOT_ROWS, LANES), 0)
    for q in range(4):
        message = jnp.zeros((SLOT_ROWS, LANES), f32)
        for c in range(4):
            turned = parts[c] if c == q else pltpu.roll(parts[c], (c - q) * CAP % LANES, 1)
            message = jnp.where(quarter == c, turned, message)
        below = jnp.where(row >= 2, pltpu.roll(message, 2, 0), 0.0)
        above = jnp.where(row < SLOT_ROWS - 2, pltpu.roll(message, SLOT_ROWS - 2, 0), 0.0)
        out_ref[pl.ds(3 * q, SLOT_ROWS, stride=12), :] = below
        out_ref[pl.ds(3 * q + 1, SLOT_ROWS, stride=12), :] = message
        out_ref[pl.ds(3 * q + 2, SLOT_ROWS, stride=12), :] = above
    for copy in copies[3:]:
        copy.wait()


def scatter_slots(gy_ref, slots_ref, source_ref, even_ref, odd_ref):
    lane = iota((SLOT_ROWS, LANES), 1)
    quarter = lane // CAP
    own_rows = CY * CX
    side_rows = CY * 2

    def unpack(k):
        parts = [jnp.zeros((SLOT_ROWS, LANES), f32) for _ in range(4)]
        for q in range(4):
            message = slots_ref[pl.ds(3 * q + k, SLOT_ROWS, stride=12), :]
            for c in range(4):
                turned = message if c == q else pltpu.roll(message, (q - c) * CAP % LANES, 1)
                parts[c] = jnp.where(quarter == q, turned, parts[c])
        ids = parts[3].astype(i32)
        pieces = []
        for c in range(3):
            pieces.extend(halves(parts[c]))
        return ids // LANES, ids % LANES, pieces

    lane_number = iota((LANES, LANES), 0)
    row_number = iota((2 * LANES, LANES), 0)
    side_number = iota((side_rows, LANES), 0)
    batch = 8
    rows, lanes, pieces = unpack(1)
    sums = jnp.zeros((6 * LANES, 2 * LANES), f32)
    for start in range(0, SLOT_ROWS, batch):
        lefts, rights = [], []
        for r in range(start, start + batch):
            here = lane_number == lanes[r : r + 1, :]
            lefts.append(jnp.concatenate([jnp.where(here, piece[r : r + 1, :], 0.0).astype(bf16) for piece in pieces], axis=0))
            rights.append(jnp.where(row_number == rows[r : r + 1, :], 1.0, 0.0).astype(bf16))
        sums = sums + dot_last(jnp.concatenate(lefts, axis=1), jnp.concatenate(rights, axis=1))
    for c in range(3):
        one = sums[2 * c * LANES : (2 * c + 1) * LANES] + sums[(2 * c + 1) * LANES : (2 * c + 2) * LANES]
        source_ref[c, 2 : 2 + CX] = jnp.transpose(one)[:own_rows].reshape(CX, CY, LANES)
    for k, first, target in ((0, own_rows - side_rows, 0), (2, 0, 2 + CX)):
        rows, lanes, pieces = unpack(k)
        sums = jnp.zeros((6 * side_rows, LANES), f32)
        for start in range(0, SLOT_ROWS, batch):
            lefts, rights = [], []
            for r in range(start, start + batch):
                here = side_number == rows[r : r + 1, :] - first
                lefts.append(jnp.concatenate([jnp.where(here, piece[r : r + 1, :], 0.0).astype(bf16) for piece in pieces], axis=0))
                rights.append(jnp.where(lane_number == lanes[r : r + 1, :], 1.0, 0.0).astype(bf16))
            sums = sums + dot_last(jnp.concatenate(lefts, axis=1), jnp.concatenate(rights, axis=1))
        for c in range(3):
            one = sums[2 * c * side_rows : (2 * c + 1) * side_rows] + sums[(2 * c + 1) * side_rows : (2 * c + 2) * side_rows]
            source_ref[c, target : target + 2] = one.reshape(2, CY, LANES)
    is_odd = lax.rem(gy_ref[0], 2) == 1
    for c in range(3):
        here = slice(2 * c, 2 * c + 2)
        first, last = source_ref[c, :, 0:2, :], source_ref[c, :, CY - 2 :, :]
        even_ref[:, here, :] = jnp.where(is_odd, first, last)
        odd_ref[:, here, :] = jnp.where(is_odd, last, first)


def pack_y(n_gx, gx_ref, gy_ref, field_hbm, stiff_hbm, mass_hbm, xeven_ref, xodd_ref, even_ref, odd_ref, ends_ref, sems):
    copies = []
    for number in range(5):
        own = field_hbm.at[number] if number < 3 else (stiff_hbm if number == 3 else mass_hbm)
        for n, rows in enumerate((pl.ds(0, 8), pl.ds(CY - 8, 8))):
            copies.append(pltpu.make_async_copy(own.at[:, rows], ends_ref.at[number, n], sems.at[len(copies)]))
    for copy in copies:
        copy.start()
    for copy in copies:
        copy.wait()
    is_odd = lax.rem(gy_ref[0], 2) == 1
    for number, (start, width) in enumerate(Y_FIELDS):
        here = slice(start, start + width)
        planes = slice(3 * number, 3 * number + 3) if number < 4 else slice(12, 14)
        pieces = [[], []]
        for n, (rows, own_rows) in enumerate(((slice(0, width), slice(0, width)), (slice(CY - width, CY), slice(8 - width, 8)))):
            low, high = by_parity((gx_ref[0], n_gx), xeven_ref[planes, rows, :], xodd_ref[planes, rows, :])
            own = ends_ref[number, n, :, own_rows, :]
            pieces[n].extend([(slice(0, 2), low[-2:]), (slice(2, 2 + CX), own), (slice(2 + CX, CX + 4), high[:2])])
        for (where, first), (_, last) in zip(*pieces):
            even_ref[where, here, :] = jnp.where(is_odd, first, last)
            odd_ref[where, here, :] = jnp.where(is_odd, last, first)


def route_hull(cells_ref, patches_ref, where_ref, ids_ref, rows_s, lanes_s):
    patches = patches_ref[...]
    cells = cells_ref[...]
    dest = patches // PATCH_BLOCK
    local = patches % PATCH_BLOCK
    hits = [jnp.where(dest == d, 1.0, 0.0) for d in range(HULL_DESTS)]
    stacked = jnp.concatenate(hits, axis=0).astype(bf16)
    upto = jnp.where(iota((LANES, LANES), 0) <= iota((LANES, LANES), 1), 1.0, 0.0).astype(bf16)
    total = HULL_DESTS * SLOT_ROWS
    within = jnp.dot(stacked, upto, preferred_element_type=f32)
    row_sums = jnp.dot(stacked, jnp.ones((LANES, LANES), bf16), preferred_element_type=f32)
    a, b = iota((total, total), 0), iota((total, total), 1)
    earlier = jnp.where((a // SLOT_ROWS == b // SLOT_ROWS) & (b < a), 1.0, 0.0).astype(bf16)
    offsets = jnp.dot(earlier, row_sums.astype(bf16), preferred_element_type=f32)
    rank = jnp.zeros((SLOT_ROWS, LANES), f32)
    for d in range(HULL_DESTS):
        cut = slice(d * SLOT_ROWS, (d + 1) * SLOT_ROWS)
        rank = rank + hits[d] * (within[cut] + offsets[cut] - 1.0)
    rank = rank.astype(i32)
    overflow = jnp.max(jnp.where(rank >= HULL_CAP, 1.0, 0.0))
    slot_row = jnp.where(rank < HULL_CAP, dest * HULL_ROWS + rank // LANES, -1)
    slot_lane = rank % LANES
    payload = [cells // LANES, cells % LANES, local // 256 + 1, local % 256]
    payload = [p.astype(f32) for p in payload]
    count = HULL_DESTS * HULL_ROWS
    row_number = iota((count, LANES), 0)
    lane_number = iota((LANES, LANES), 0)
    for r in range(SLOT_ROWS):
        cut = slice(r * LANES, (r + 1) * LANES)
        here = row_number == slot_row[r : r + 1, :]
        for n in range(4):
            rows_s[n * count : (n + 1) * count, cut] = jnp.where(here, payload[n][r : r + 1, :], 0.0).astype(bf16)
        lanes_s[:, cut] = jnp.where(lane_number == slot_lane[r : r + 1, :], 1.0, 0.0).astype(bf16)
    placed = dot_last(rows_s[...], lanes_s[...])
    where_ref[...] = placed[: 2 * count].astype(i32)
    ids = jnp.maximum((placed[2 * count : 3 * count] - 1.0) * 256.0 + placed[3 * count :] + 1.0, 0.0)
    last = (iota((count, LANES), 1) == LANES - 1) & (row_number % HULL_ROWS == HULL_ROWS - 1)
    ids_ref[...] = jnp.where(last, overflow, ids)


def pack_z(side, arrays, z_ref):
    lane = iota((1, 1, LANES), 2)
    total = jnp.zeros((EXT_X - 2, EXT_Y, LANES), f32)
    for number, array in enumerate(arrays):
        shift = jnp.where(side == 0, (3 * number + 3) % LANES, 3 * number)
        turned = pltpu.roll(array.reshape((EXT_X - 2) * EXT_Y, LANES), shift, 1).reshape(EXT_X - 2, EXT_Y, LANES)
        total = jnp.where((lane >= 3 * number) & (lane < 3 * number + 3), turned, total)
    z_ref[...] = jnp.transpose(total.reshape((EXT_X - 2) * EXT_Y, LANES))[:Z_ROWS]


def unpack_z(side, z_ref):
    rows = (EXT_X - 2) * EXT_Y
    lane = iota((1, 1, LANES), 2)
    columns = jnp.transpose(jnp.concatenate([z_ref[...], jnp.zeros((LANES - Z_ROWS, rows), f32)], axis=0))
    first_lane = jnp.where(side == 0, 0, LANES - 3)
    near = (lane >= first_lane) & (lane < first_lane + 3)

    def beyond(number):
        shift = jnp.where(side == 0, (LANES - 3 * number) % LANES, (2 * LANES - 3 - 3 * number) % LANES)
        return jnp.where(near, pltpu.roll(columns, shift, 1).reshape(EXT_X - 2, EXT_Y, LANES), 0.0)

    return beyond


def widen_fixed(n_gx, n_gy, gx_ref, gy_ref, side_ref, field_ref, stiff_ref, mass_ref, xeven_ref, xodd_ref, yeven_ref, yodd_ref, ext_ref, z_ref):
    zeros = jnp.zeros((EXT_X, EXT_Y - CY, LANES), f32)
    for number, (start, width) in enumerate(Y_FIELDS):
        target = ext_ref.at[number]
        target[:, CY:, :] = zeros
        planes = slice(3 * number, 3 * number + 3) if number < 4 else slice(12, 14)
        low, high = by_parity((gx_ref[0], n_gx), xeven_ref[planes], xodd_ref[planes])
        own = field_ref.at[number] if number < 3 else (stiff_ref if number == 3 else mass_ref)
        if width < 3:
            target[0, :CY, :] = jnp.zeros((CY, LANES), f32)
            target[EXT_X - 1, :CY, :] = jnp.zeros((CY, LANES), f32)
        target[3 - width : 3, :CY, :] = low
        target[3 : 3 + CX, :CY, :] = own[...]
        target[3 + CX : 3 + CX + width, :CY, :] = high
        here = slice(start, start + width)
        low, high = by_parity((gy_ref[0], n_gy), yeven_ref[:, here, :], yodd_ref[:, here, :])
        target[1 : EXT_X - 1, CY : CY + width, :] = high
        target[1 : EXT_X - 1, EXT_Y - width :, :] = low
    pack_z(side_ref[0], [ext_ref[number, 1 : EXT_X - 1] for number in range(5)], z_ref)


def widen_source(n_gy, gy_ref, side_ref, source_ref, yeven_ref, yodd_ref, ext_ref, z_ref):
    zeros = jnp.zeros((EXT_X - 2, EXT_Y - CY, LANES), f32)
    for c in range(3):
        here = slice(2 * c, 2 * c + 2)
        low, high = by_parity((gy_ref[0], n_gy), yeven_ref[:, here, :], yodd_ref[:, here, :])
        ext_ref[c, :, CY:, :] = zeros
        ext_ref[c, :, :CY, :] = source_ref[c]
        ext_ref[c, :, CY : CY + 2, :] = high
        ext_ref[c, :, EXT_Y - 2 :, :] = low
    pack_z(side_ref[0], [ext_ref[c] for c in range(3)], z_ref)


def around(ref_at, x):
    middle = ref_at(x)
    return middle, (
        ref_at(x + 1),
        ref_at(x - 1),
        pltpu.roll(middle, EXT_Y - 1, 0),
        pltpu.roll(middle, 1, 0),
        pltpu.roll(middle, 2 * LANES - 1, 1),
        pltpu.roll(middle, 1, 1),
    )


def prepare(side_ref, ext_ref, z_ref, start_ref, weight_ref, keep_ref, couple_ref, rate_ref, stiff_s, mass_s):
    beyond = unpack_z(side_ref[0], z_ref)
    empty = jnp.zeros((EXT_Y, LANES), f32)
    for c in range(3):
        start_ref[c, :, :, :LANES] = ext_ref[c]
        start_ref[c, 1 : EXT_X - 1, :, LANES:] = beyond(c)
        start_ref[c, 0, :, LANES:] = empty
        start_ref[c, EXT_X - 1, :, LANES:] = empty
    stiff_s[:, :, :LANES] = ext_ref[3]
    stiff_s[1 : EXT_X - 1, :, LANES:] = beyond(3)
    stiff_s[0, :, LANES:] = empty
    stiff_s[EXT_X - 1, :, LANES:] = empty
    mass_s[:, :, :LANES] = ext_ref[4, 1 : EXT_X - 1]
    mass_s[:, :, LANES:] = beyond(4)

    def one(i, carry):
        middle, others = around(lambda x: stiff_s[x], i + 1)
        weights = [0.5 * (middle + other) for other in others]
        weight_sum = weights[0] + weights[1] + weights[2] + weights[3] + weights[4] + weights[5]
        mass = mass_s[i]
        inside = middle > 0.0
        rate = jnp.where(inside, RELAX / jnp.where(inside, weight_sum + 1.25 * mass, 1.0), 0.0)
        for n in range(6):
            weight_ref[n, i] = rate * weights[n]
        keep_ref[i] = jnp.where(inside, 1.0 - rate * (weight_sum + mass), 0.0)
        couple_ref[i] = 0.25 * rate * mass
        rate_ref[i] = rate
        return carry

    lax.fori_loop(0, EXT_X - 2, one, 0)


def relax_and_gather(
    side_ref,
    start_ref,
    weight_s,
    keep_s,
    couple_s,
    rate_ref,
    ext_ref,
    z_ref,
    stiff_ref,
    where_ref,
    ids_ref,
    out_ref,
    message_ref,
    first_s,
    second_s,
    push_s,
    pieces_s,
):
    beyond = unpack_z(side_ref[0], z_ref)
    for c in range(3):
        push_s[c, :, :, :LANES] = rate_ref[:, :, :LANES] * ext_ref[c]
        push_s[c, :, :, LANES:] = rate_ref[:, :, LANES:] * beyond(c)

    def sweep(source, target, lowest, highest):
        def one(x, carry):
            i = x - 1
            gathered = [around(lambda y, c=c: source[c, y], x) for c in range(3)]
            shared = couple_s[i] * (gathered[0][0] + gathered[1][0] + gathered[2][0])
            for c in range(3):
                middle, others = gathered[c]
                value = keep_s[i] * middle + (push_s[c, i] - shared)
                for n in range(6):
                    value = value + weight_s[n, i] * others[n]
                target[c, x] = value
            return carry

        lax.fori_loop(lowest, highest, one, 0)

    sweep(start_ref, second_s, 1, EXT_X - 1)
    sweep(second_s, first_s, 2, EXT_X - 2)

    def finish(x, carry):
        i = x - 1
        middles = [first_s[c, x, :CY, :LANES] for c in range(3)]
        shared = couple_s[i, :CY, :LANES] * (middles[0] + middles[1] + middles[2])
        for c in range(3):
            columns = first_s[c, x, :, :LANES]
            halo = first_s[c, x, :CY, LANES:]
            others = (
                first_s[c, x + 1, :CY, :LANES],
                first_s[c, x - 1, :CY, :LANES],
                pltpu.roll(columns, EXT_Y - 1, 0)[:CY],
                pltpu.roll(columns, 1, 0)[:CY],
                pltpu.roll(jnp.where(last_lane == 0, halo, middles[c]), LANES - 1, 1),
                pltpu.roll(jnp.where(last_lane == LANES - 1, halo, middles[c]), 1, 1),
            )
            value = keep_s[i, :CY, :LANES] * middles[c] + (push_s[c, i, :CY, :LANES] - shared)
            for n in range(6):
                value = value + weight_s[n, i, :CY, :LANES] * others[n]
            out_ref[c, x - 3] = value
        return carry

    last_lane = iota((CY, LANES), 1)
    lax.fori_loop(3, 3 + CX, finish, 0)

    own_rows = CX * CY
    for c in range(3):
        scaled = (out_ref[c] * stiff_ref[...]).reshape(own_rows, LANES)
        for n, piece in enumerate(halves(scaled)):
            pieces_s[c * own_rows : (c + 1) * own_rows, n * LANES : (n + 1) * LANES] = piece.astype(bf16)
    count = HULL_DESTS * HULL_ROWS
    row_number = iota((own_rows, LANES), 0)
    lane_number = iota((LANES, LANES), 0)
    group = 2 * HULL_ROWS
    for g in range(count // group):
        chosen = []
        for r in range(g * group, (g + 1) * group):
            chosen.append(jnp.where(lane_number == where_ref[count + r : count + r + 1, :], 1.0, 0.0).astype(bf16))
        chosen = jnp.concatenate(chosen, axis=1)
        found = jnp.dot(pieces_s[...], jnp.concatenate([chosen, chosen], axis=0), preferred_element_type=f32)
        for i in range(group):
            r = g * group + i
            here = row_number == where_ref[r : r + 1, :]
            base = r // HULL_ROWS * 4 * HULL_ROWS + r % HULL_ROWS
            for c in range(3):
                part = found[c * own_rows : (c + 1) * own_rows, i * LANES : (i + 1) * LANES]
                spot = base + c * HULL_ROWS
                message_ref[spot : spot + 1, :] = jnp.sum(jnp.where(here, part, 0.0), axis=0, keepdims=True)
            spot = base + 3 * HULL_ROWS
            message_ref[spot : spot + 1, :] = ids_ref[r : r + 1, :]


def scatter_hull(nodes_ref, out_hbm, overflow_ref, out_ref, sem):
    flags = nodes_ref[pl.ds(4 * HULL_ROWS - 1, HULL_DESTS, stride=4 * HULL_ROWS), :]
    last = iota((HULL_DESTS, LANES), 1) == LANES - 1
    overflow_ref[0] = jnp.max(jnp.where(last, flags, 0.0)).astype(i32)
    row_number = iota((64, LANES), 0)
    column_number = iota((256, LANES), 0)
    sums = jnp.zeros((6 * 64, 256), f32)
    batch = 4
    for first in range(0, HULL_DESTS, batch):
        lefts, rights = [], []
        for n in range(batch * HULL_ROWS):
            base = (first + n // HULL_ROWS) * 4 * HULL_ROWS + n % HULL_ROWS
            ids = nodes_ref[base + 3 * HULL_ROWS : base + 3 * HULL_ROWS + 1, :].astype(i32) - 1
            here = row_number == (ids >> 8)
            pieces = []
            for c in range(3):
                values = nodes_ref[base + c * HULL_ROWS : base + c * HULL_ROWS + 1, :]
                pieces.extend(jnp.where(here, part, 0.0).astype(bf16) for part in halves(values))
            lefts.append(jnp.concatenate(pieces, axis=0))
            rights.append(jnp.where(column_number == (ids & 255), 1.0, 0.0).astype(bf16))
        sums = sums + dot_last(jnp.concatenate(lefts, axis=1), jnp.concatenate(rights, axis=1))
    for c in range(3):
        out_ref[c] = sums[2 * c * 64 : (2 * c + 1) * 64] + sums[(2 * c + 1) * 64 : (2 * c + 2) * 64]
    copy = pltpu.make_async_copy(out_ref, out_hbm, sem)
    copy.start()
    copy.wait()


def shaped(*shape, dtype=f32):
    return jax.ShapeDtypeStruct(shape, dtype)


def call(kernel, outs, scratch, cost, *args, places="", out_places=""):
    spaces = {"V": pltpu.VMEM, "S": pltpu.SMEM, "H": pltpu.HBM}

    def specs(count, names):
        names = names + "V" * (count - len(names))
        return [pl.BlockSpec(memory_space=spaces[name]) for name in names]

    args = [pltpu.with_memory_space_constraint(arg, pltpu.HBM) if place == "H" else arg for arg, place in zip(args, places + "V" * len(args))]
    if isinstance(outs, tuple):
        outs = tuple(pltpu.HBM(out.shape, out.dtype) if place == "H" else out for out, place in zip(outs, out_places + "V" * len(outs)))
    return pl.pallas_call(
        kernel,
        out_shape=outs,
        in_specs=specs(len(args), places),
        out_specs=tuple(specs(len(outs), out_places)) if isinstance(outs, tuple) else specs(1, out_places)[0],
        scratch_shapes=scratch,
        compiler_params=PARAMS,
        cost_estimate=pl.CostEstimate(flops=cost, bytes_accessed=1 << 20, transcendentals=0),
        name=getattr(kernel, "func", kernel).__name__,
    )(*args)


def pair_exchange(axis, even, odd):
    count = lax.axis_size(axis)
    results = []
    for first, values in ((0, even), (1, odd)):
        pairs = [(i, (i + 1) % count) for i in range(first, count, 2)]
        results.append(lax.ppermute(values, axis, pairs + [(b, a) for a, b in pairs]))
    return results


def per_device(start_field, stiffness, mass, sens_values, sens_cells, sens_counts, hull_cells, hull_patches):
    slabs = shaped(14, CY, CZ)
    gx, gy, side = (lax.axis_index(axis).astype(i32).reshape(1) for axis in ("gx", "gy", "gz"))
    packed, even, odd = call(
        pack_slots,
        (shaped(3 * BLOCKS, LANES), slabs, slabs),
        [
            pltpu.VMEM((3, SLOT_ROWS, LANES), f32),
            pltpu.VMEM((SLOT_ROWS, LANES), i32),
            pltpu.VMEM((1, BLOCKS), i32),
            pltpu.SemaphoreType.DMA((13,)),
        ],
        1 << 20,
        gx,
        sens_values.reshape(3, SLOT_ROWS, LANES),
        sens_cells.reshape(SLOT_ROWS, LANES),
        sens_counts.reshape(1, BLOCKS),
        start_field,
        stiffness,
        mass,
        places="SHHHHHH",
    )
    packed = packed.reshape(BLOCKS, 1, 3 * LANES)
    arrived = lax.all_to_all(packed, ("gx", "gy"), split_axis=0, concat_axis=0, tiled=True)
    xeven, xodd = pair_exchange("gx", even, odd)
    count = HULL_DESTS * HULL_ROWS
    where, ids = call(
        route_hull,
        (shaped(2 * count, LANES, dtype=i32), shaped(count, LANES)),
        [pltpu.VMEM((4 * count, SLOTS), bf16), pltpu.VMEM((LANES, SLOTS), bf16)],
        1 << 31,
        hull_cells.reshape(SLOT_ROWS, LANES),
        hull_patches.reshape(SLOT_ROWS, LANES),
    )
    n_gx, n_gy = lax.axis_size("gx"), lax.axis_size("gy")
    y_message = shaped(CX + 4, Y_ROWS, CZ)
    even, odd = call(
        functools.partial(pack_y, n_gx),
        (y_message, y_message),
        [pltpu.VMEM((5, 2, CX, 8, CZ), f32), pltpu.SemaphoreType.DMA((10,))],
        1 << 34,
        gx,
        gy,
        start_field,
        stiffness,
        mass,
        xeven,
        xodd,
        places="SSHHH",
    )
    yeven, yodd = pair_exchange("gy", even, odd)
    arrived, yeven, yodd = lax.optimization_barrier((arrived, yeven, yodd))
    y_message = shaped(CX + 4, 6, CZ)
    source, even, odd = call(
        scatter_slots,
        (shaped(3, CX + 4, CY, CZ), y_message, y_message),
        [],
        1 << 32,
        gy,
        arrived.reshape(3 * BLOCKS, LANES),
        places="S",
    )
    rows = (EXT_X - 2) * EXT_Y
    z_message = shaped(Z_ROWS, rows)
    source_even, source_odd = pair_exchange("gy", even, odd)
    ext, faces = call(
        functools.partial(widen_fixed, n_gx, n_gy),
        (shaped(5, EXT_X, EXT_Y, CZ), z_message),
        [],
        1 << 20,
        gx,
        gy,
        side,
        start_field,
        stiffness,
        mass,
        xeven,
        xodd,
        yeven,
        yodd,
        places="SSS",
    )
    faces = lax.ppermute(faces, "gz", [(0, 1), (1, 0)])
    source_ext, source_faces = call(
        functools.partial(widen_source, n_gy),
        (shaped(3, EXT_X - 2, EXT_Y, CZ), z_message),
        [],
        1 << 20,
        gy,
        side,
        source,
        source_even,
        source_odd,
        places="SS",
    )
    source_faces = lax.ppermute(source_faces, "gz", [(0, 1), (1, 0)])
    wide = (EXT_X - 2, EXT_Y, 2 * CZ)
    full = (EXT_X, EXT_Y, 2 * CZ)
    prepared = call(
        prepare,
        (shaped(3, *full), shaped(6, *wide), shaped(*wide), shaped(*wide), shaped(*wide)),
        [pltpu.VMEM(full, f32), pltpu.VMEM(wide, f32)],
        1 << 30,
        side,
        ext,
        faces,
        places="S",
    )
    field, outgoing = call(
        relax_and_gather,
        (shaped(3, CX, CY, CZ), shaped(4 * count, LANES)),
        [
            pltpu.VMEM((3,) + full, f32),
            pltpu.VMEM((3,) + full, f32),
            pltpu.VMEM((3,) + wide, f32),
            pltpu.VMEM((3 * CX * CY, 2 * LANES), bf16),
        ],
        1 << 32,
        side,
        *prepared,
        source_ext,
        source_faces,
        stiffness,
        where,
        ids,
        places="S",
    )
    outgoing = outgoing.reshape(HULL_DESTS, 1, 4 * HULL_ROWS * LANES)
    nodes = lax.all_to_all(outgoing, ("gy", "gz"), split_axis=0, concat_axis=0, tiled=True)
    nodes = nodes.reshape(4 * count, LANES)
    patch, overflow = call(
        scatter_hull,
        (shaped(3, 64, 256), shaped(1, dtype=i32)),
        [pltpu.VMEM((3, 64, 256), f32), pltpu.SemaphoreType.DMA],
        1 << 32,
        nodes,
        out_places="HS",
    )

    def in_messages():
        return patch

    def every_node():
        cells = hull_cells[0, 0]
        values = field.reshape(3, -1)[:, cells] * stiffness.reshape(-1)[cells]
        sent = jnp.concatenate([values, hull_patches[0].astype(f32)], axis=0)
        sent = jnp.broadcast_to(sent[None], (HULL_DESTS,) + sent.shape)
        got = lax.all_to_all(sent, ("gy", "gz"), split_axis=0, concat_axis=0, tiled=True)
        got = jnp.swapaxes(got, 0, 1).reshape(4, -1)
        spots = got[3].astype(i32) - lax.axis_index(("gy", "gz")) * PATCH_BLOCK
        mine = (spots >= 0) & (spots < PATCH_BLOCK)
        added = jnp.where(mine, got[:3], 0.0)
        patch = jnp.zeros((3, PATCH_BLOCK), f32).at[:, jnp.where(mine, spots, 0)].add(added)
        return patch.reshape(3, 64, 256)

    patch = lax.cond(overflow[0] > 0, every_node, in_messages)
    return field, patch


def solution(mesh):
    placed = (
        P(None, "gx", "gy", "gz"),
        P("gx", "gy", "gz"),
        P("gx", "gy", "gz"),
        P(None, "gz", ("gx", "gy"), None),
        P("gz", ("gx", "gy"), None),
        P("gz", ("gx", "gy"), None),
        P("gx", ("gy", "gz"), None),
        P("gx", ("gy", "gz"), None),
    )
    return jax.shard_map(
        per_device,
        mesh=mesh,
        in_specs=placed,
        out_specs=(P(None, "gx", "gy", "gz"), P(None, ("gy", "gz"), "gx")),
        check_vma=False,
    )
```

```python
import functools

import jax
import jax.numpy as jnp
from jax import lax
from jax.experimental import pallas as pl
from jax.experimental.pallas import tpu as pltpu
from jax.sharding import PartitionSpec as P

CX, CY, CZ = 8, 24, 128
LANES = 128
SLOTS = 4096
SLOT_ROWS = SLOTS // LANES
BLOCKS = 128
CAP = 32
HULL_DESTS = 16
PATCH_BLOCK = 64 * 256
HULL_ROWS = 3
HULL_CAP = HULL_ROWS * LANES - 1
Y_ROWS = 14
Y_FIELDS = ((0, 3), (3, 3), (6, 3), (9, 3), (12, 2))
Z_ROWS = 16
EXT_X = CX + 6
EXT_Y = 32
RELAX = 0.8

f32, bf16, i32 = jnp.float32, jnp.bfloat16, jnp.int32
PARAMS = pltpu.CompilerParams(vmem_limit_bytes=24 * 1024 * 1024)


def iota(shape, dim):
    return lax.broadcasted_iota(i32, shape, dim)


def halves(values):
    high = values.astype(bf16).astype(f32)
    return high, values - high


def dot_last(a, b):
    return lax.dot_general(a, b, (((1,), (1,)), ((), ())), preferred_element_type=f32)


def by_parity(place, even, odd):
    index, count = place
    is_odd = lax.rem(index, 2) == 1
    low = jnp.where(is_odd, even, odd) * jnp.where(index > 0, 1.0, 0.0)
    high = jnp.where(is_odd, odd, even) * jnp.where(index < count - 1, 1.0, 0.0)
    return low, high


def pack_slots(
    gx_ref, values_hbm, cells_hbm, counts_hbm, field_hbm, stiff_hbm, mass_hbm, out_ref, even_ref, odd_ref, values_ref, cells_ref, counts_ref, sems
):
    copies = [
        pltpu.make_async_copy(values_hbm, values_ref, sems.at[0]),
        pltpu.make_async_copy(cells_hbm, cells_ref, sems.at[1]),
        pltpu.make_async_copy(counts_hbm, counts_ref, sems.at[2]),
    ]
    odd = lax.rem(gx_ref[0], 2)
    for slab, up in ((even_ref, 1 - odd), (odd_ref, odd)):
        planes, mass_planes = pl.ds(up * (CX - 3), 3), pl.ds(up * (CX - 2), 2)
        for c in range(3):
            copies.append(pltpu.make_async_copy(field_hbm.at[c, planes], slab.at[pl.ds(3 * c, 3)], sems.at[len(copies)]))
        copies.append(pltpu.make_async_copy(stiff_hbm.at[planes], slab.at[pl.ds(9, 3)], sems.at[len(copies)]))
        copies.append(pltpu.make_async_copy(mass_hbm.at[mass_planes], slab.at[pl.ds(12, 2)], sems.at[len(copies)]))
    for copy in copies:
        copy.start()
    for copy in copies[:3]:
        copy.wait()
    counts = counts_ref[...].astype(f32)
    spread = jnp.where(iota((SLOT_ROWS, BLOCKS), 1) // 4 == iota((SLOT_ROWS, BLOCKS), 0), counts, 0.0)
    place = jnp.where(iota((BLOCKS, LANES), 0) % 4 == iota((BLOCKS, LANES), 1) // CAP, 1.0, 0.0)
    limits = jnp.dot(spread.astype(bf16), place.astype(bf16), preferred_element_type=f32)
    lane = iota((SLOT_ROWS, LANES), 1)
    live = (lane % CAP).astype(f32) < limits
    parts = [jnp.where(live, values_ref[c], 0.0) for c in range(3)] + [cells_ref[...].astype(f32)]
    quarter = lane // CAP
    row = iota((SLOT_ROWS, LANES), 0)
    for q in range(4):
        message = jnp.zeros((SLOT_ROWS, LANES), f32)
        for c in range(4):
            turned = parts[c] if c == q else pltpu.roll(parts[c], (c - q) * CAP % LANES, 1)
            message = jnp.where(quarter == c, turned, message)
        below = jnp.where(row >= 2, pltpu.roll(message, 2, 0), 0.0)
        above = jnp.where(row < SLOT_ROWS - 2, pltpu.roll(message, SLOT_ROWS - 2, 0), 0.0)
        out_ref[pl.ds(3 * q, SLOT_ROWS, stride=12), :] = below
        out_ref[pl.ds(3 * q + 1, SLOT_ROWS, stride=12), :] = message
        out_ref[pl.ds(3 * q + 2, SLOT_ROWS, stride=12), :] = above
    for copy in copies[3:]:
        copy.wait()


def scatter_slots(gy_ref, slots_ref, source_ref, even_ref, odd_ref):
    lane = iota((SLOT_ROWS, LANES), 1)
    quarter = lane // CAP
    own_rows = CY * CX
    side_rows = CY * 2

    def unpack(k):
        parts = [jnp.zeros((SLOT_ROWS, LANES), f32) for _ in range(4)]
        for q in range(4):
            message = slots_ref[pl.ds(3 * q + k, SLOT_ROWS, stride=12), :]
            for c in range(4):
                turned = message if c == q else pltpu.roll(message, (q - c) * CAP % LANES, 1)
                parts[c] = jnp.where(quarter == q, turned, parts[c])
        ids = parts[3].astype(i32)
        pieces = []
        for c in range(3):
            pieces.extend(halves(parts[c]))
        return ids // LANES, ids % LANES, pieces

    lane_number = iota((LANES, LANES), 0)
    row_number = iota((2 * LANES, LANES), 0)
    side_number = iota((side_rows, LANES), 0)
    batch = 8
    rows, lanes, pieces = unpack(1)
    sums = jnp.zeros((6 * LANES, 2 * LANES), f32)
    for start in range(0, SLOT_ROWS, batch):
        lefts, rights = [], []
        for r in range(start, start + batch):
            here = lane_number == lanes[r : r + 1, :]
            lefts.append(jnp.concatenate([jnp.where(here, piece[r : r + 1, :], 0.0).astype(bf16) for piece in pieces], axis=0))
            rights.append(jnp.where(row_number == rows[r : r + 1, :], 1.0, 0.0).astype(bf16))
        sums = sums + dot_last(jnp.concatenate(lefts, axis=1), jnp.concatenate(rights, axis=1))
    for c in range(3):
        one = sums[2 * c * LANES : (2 * c + 1) * LANES] + sums[(2 * c + 1) * LANES : (2 * c + 2) * LANES]
        source_ref[c, 2 : 2 + CX] = jnp.transpose(one)[:own_rows].reshape(CX, CY, LANES)
    for k, first, target in ((0, own_rows - side_rows, 0), (2, 0, 2 + CX)):
        rows, lanes, pieces = unpack(k)
        sums = jnp.zeros((6 * side_rows, LANES), f32)
        for start in range(0, SLOT_ROWS, batch):
            lefts, rights = [], []
            for r in range(start, start + batch):
                here = side_number == rows[r : r + 1, :] - first
                lefts.append(jnp.concatenate([jnp.where(here, piece[r : r + 1, :], 0.0).astype(bf16) for piece in pieces], axis=0))
                rights.append(jnp.where(lane_number == lanes[r : r + 1, :], 1.0, 0.0).astype(bf16))
            sums = sums + dot_last(jnp.concatenate(lefts, axis=1), jnp.concatenate(rights, axis=1))
        for c in range(3):
            one = sums[2 * c * side_rows : (2 * c + 1) * side_rows] + sums[(2 * c + 1) * side_rows : (2 * c + 2) * side_rows]
            source_ref[c, target : target + 2] = one.reshape(2, CY, LANES)
    is_odd = lax.rem(gy_ref[0], 2) == 1
    for c in range(3):
        here = slice(2 * c, 2 * c + 2)
        first, last = source_ref[c, :, 0:2, :], source_ref[c, :, CY - 2 :, :]
        even_ref[:, here, :] = jnp.where(is_odd, first, last)
        odd_ref[:, here, :] = jnp.where(is_odd, last, first)


def pack_y(n_gx, gx_ref, gy_ref, field_hbm, stiff_hbm, mass_hbm, xeven_ref, xodd_ref, even_ref, odd_ref, ends_ref, sems):
    copies = []
    for number in range(5):
        own = field_hbm.at[number] if number < 3 else (stiff_hbm if number == 3 else mass_hbm)
        for n, rows in enumerate((pl.ds(0, 8), pl.ds(CY - 8, 8))):
            copies.append(pltpu.make_async_copy(own.at[:, rows], ends_ref.at[number, n], sems.at[len(copies)]))
    for copy in copies:
        copy.start()
    for copy in copies:
        copy.wait()
    is_odd = lax.rem(gy_ref[0], 2) == 1
    for number, (start, width) in enumerate(Y_FIELDS):
        here = slice(start, start + width)
        planes = slice(3 * number, 3 * number + 3) if number < 4 else slice(12, 14)
        pieces = [[], []]
        for n, (rows, own_rows) in enumerate(((slice(0, width), slice(0, width)), (slice(CY - width, CY), slice(8 - width, 8)))):
            low, high = by_parity((gx_ref[0], n_gx), xeven_ref[planes, rows, :], xodd_ref[planes, rows, :])
            own = ends_ref[number, n, :, own_rows, :]
            pieces[n].extend([(slice(0, 2), low[-2:]), (slice(2, 2 + CX), own), (slice(2 + CX, CX + 4), high[:2])])
        for (where, first), (_, last) in zip(*pieces):
            even_ref[where, here, :] = jnp.where(is_odd, first, last)
            odd_ref[where, here, :] = jnp.where(is_odd, last, first)


def route_hull(cells_ref, patches_ref, where_ref, ids_ref, rows_s, lanes_s):
    patches = patches_ref[...]
    cells = cells_ref[...]
    dest = patches // PATCH_BLOCK
    local = patches % PATCH_BLOCK
    hits = [jnp.where(dest == d, 1.0, 0.0) for d in range(HULL_DESTS)]
    stacked = jnp.concatenate(hits, axis=0).astype(bf16)
    upto = jnp.where(iota((LANES, LANES), 0) <= iota((LANES, LANES), 1), 1.0, 0.0).astype(bf16)
    total = HULL_DESTS * SLOT_ROWS
    within = jnp.dot(stacked, upto, preferred_element_type=f32)
    row_sums = jnp.dot(stacked, jnp.ones((LANES, LANES), bf16), preferred_element_type=f32)
    a, b = iota((total, total), 0), iota((total, total), 1)
    earlier = jnp.where((a // SLOT_ROWS == b // SLOT_ROWS) & (b < a), 1.0, 0.0).astype(bf16)
    offsets = jnp.dot(earlier, row_sums.astype(bf16), preferred_element_type=f32)
    rank = jnp.zeros((SLOT_ROWS, LANES), f32)
    for d in range(HULL_DESTS):
        cut = slice(d * SLOT_ROWS, (d + 1) * SLOT_ROWS)
        rank = rank + hits[d] * (within[cut] + offsets[cut] - 1.0)
    rank = rank.astype(i32)
    overflow = jnp.max(jnp.where(rank >= HULL_CAP, 1.0, 0.0))
    slot_row = jnp.where(rank < HULL_CAP, dest * HULL_ROWS + rank // LANES, -1)
    slot_lane = rank % LANES
    payload = [cells // LANES, cells % LANES, local // 256 + 1, local % 256]
    payload = [p.astype(f32) for p in payload]
    count = HULL_DESTS * HULL_ROWS
    row_number = iota((count, LANES), 0)
    lane_number = iota((LANES, LANES), 0)
    for r in range(SLOT_ROWS):
        cut = slice(r * LANES, (r + 1) * LANES)
        here = row_number == slot_row[r : r + 1, :]
        for n in range(4):
            rows_s[n * count : (n + 1) * count, cut] = jnp.where(here, payload[n][r : r + 1, :], 0.0).astype(bf16)
        lanes_s[:, cut] = jnp.where(lane_number == slot_lane[r : r + 1, :], 1.0, 0.0).astype(bf16)
    placed = dot_last(rows_s[...], lanes_s[...])
    where_ref[...] = placed[: 2 * count].astype(i32)
    ids = jnp.maximum((placed[2 * count : 3 * count] - 1.0) * 256.0 + placed[3 * count :] + 1.0, 0.0)
    last = (iota((count, LANES), 1) == LANES - 1) & (row_number % HULL_ROWS == HULL_ROWS - 1)
    ids_ref[...] = jnp.where(last, overflow, ids)


def pack_z(side, arrays, z_ref):
    lane = iota((1, 1, LANES), 2)
    total = jnp.zeros((EXT_X - 2, EXT_Y, LANES), f32)
    for number, array in enumerate(arrays):
        shift = jnp.where(side == 0, (3 * number + 3) % LANES, 3 * number)
        turned = pltpu.roll(array.reshape((EXT_X - 2) * EXT_Y, LANES), shift, 1).reshape(EXT_X - 2, EXT_Y, LANES)
        total = jnp.where((lane >= 3 * number) & (lane < 3 * number + 3), turned, total)
    z_ref[...] = jnp.transpose(total.reshape((EXT_X - 2) * EXT_Y, LANES))[:Z_ROWS]


def unpack_z(side, z_ref):
    rows = (EXT_X - 2) * EXT_Y
    lane = iota((1, 1, LANES), 2)
    columns = jnp.transpose(jnp.concatenate([z_ref[...], jnp.zeros((LANES - Z_ROWS, rows), f32)], axis=0))
    first_lane = jnp.where(side == 0, 0, LANES - 3)
    near = (lane >= first_lane) & (lane < first_lane + 3)

    def beyond(number):
        shift = jnp.where(side == 0, (LANES - 3 * number) % LANES, (2 * LANES - 3 - 3 * number) % LANES)
        return jnp.where(near, pltpu.roll(columns, shift, 1).reshape(EXT_X - 2, EXT_Y, LANES), 0.0)

    return beyond


def widen_fixed(n_gx, n_gy, gx_ref, gy_ref, side_ref, field_ref, stiff_ref, mass_ref, xeven_ref, xodd_ref, yeven_ref, yodd_ref, ext_ref, z_ref):
    zeros = jnp.zeros((EXT_X, EXT_Y - CY, LANES), f32)
    for number, (start, width) in enumerate(Y_FIELDS):
        target = ext_ref.at[number]
        target[:, CY:, :] = zeros
        planes = slice(3 * number, 3 * number + 3) if number < 4 else slice(12, 14)
        low, high = by_parity((gx_ref[0], n_gx), xeven_ref[planes], xodd_ref[planes])
        own = field_ref.at[number] if number < 3 else (stiff_ref if number == 3 else mass_ref)
        if width < 3:
            target[0, :CY, :] = jnp.zeros((CY, LANES), f32)
            target[EXT_X - 1, :CY, :] = jnp.zeros((CY, LANES), f32)
        target[3 - width : 3, :CY, :] = low
        target[3 : 3 + CX, :CY, :] = own[...]
        target[3 + CX : 3 + CX + width, :CY, :] = high
        here = slice(start, start + width)
        low, high = by_parity((gy_ref[0], n_gy), yeven_ref[:, here, :], yodd_ref[:, here, :])
        target[1 : EXT_X - 1, CY : CY + width, :] = high
        target[1 : EXT_X - 1, EXT_Y - width :, :] = low
    pack_z(side_ref[0], [ext_ref[number, 1 : EXT_X - 1] for number in range(5)], z_ref)


def widen_source(n_gy, gy_ref, side_ref, source_ref, yeven_ref, yodd_ref, ext_ref, z_ref):
    zeros = jnp.zeros((EXT_X - 2, EXT_Y - CY, LANES), f32)
    for c in range(3):
        here = slice(2 * c, 2 * c + 2)
        low, high = by_parity((gy_ref[0], n_gy), yeven_ref[:, here, :], yodd_ref[:, here, :])
        ext_ref[c, :, CY:, :] = zeros
        ext_ref[c, :, :CY, :] = source_ref[c]
        ext_ref[c, :, CY : CY + 2, :] = high
        ext_ref[c, :, EXT_Y - 2 :, :] = low
    pack_z(side_ref[0], [ext_ref[c] for c in range(3)], z_ref)


def around(ref_at, x):
    middle = ref_at(x)
    return middle, (
        ref_at(x + 1),
        ref_at(x - 1),
        pltpu.roll(middle, EXT_Y - 1, 0),
        pltpu.roll(middle, 1, 0),
        pltpu.roll(middle, 2 * LANES - 1, 1),
        pltpu.roll(middle, 1, 1),
    )


def prepare(side_ref, ext_ref, z_ref, start_ref, weight_ref, keep_ref, couple_ref, rate_ref, stiff_s, mass_s):
    beyond = unpack_z(side_ref[0], z_ref)
    empty = jnp.zeros((EXT_Y, LANES), f32)
    for c in range(3):
        start_ref[c, :, :, :LANES] = ext_ref[c]
        start_ref[c, 1 : EXT_X - 1, :, LANES:] = beyond(c)
        start_ref[c, 0, :, LANES:] = empty
        start_ref[c, EXT_X - 1, :, LANES:] = empty
    stiff_s[:, :, :LANES] = ext_ref[3]
    stiff_s[1 : EXT_X - 1, :, LANES:] = beyond(3)
    stiff_s[0, :, LANES:] = empty
    stiff_s[EXT_X - 1, :, LANES:] = empty
    mass_s[:, :, :LANES] = ext_ref[4, 1 : EXT_X - 1]
    mass_s[:, :, LANES:] = beyond(4)

    def one(i):
        middle, others = around(lambda x: stiff_s[x], i + 1)
        weights = [0.5 * (middle + other) for other in others]
        weight_sum = weights[0] + weights[1] + weights[2] + weights[3] + weights[4] + weights[5]
        mass = mass_s[i]
        inside = middle > 0.0
        rate = jnp.where(inside, RELAX / jnp.where(inside, weight_sum + 1.25 * mass, 1.0), 0.0)
        for n in range(6):
            weight_ref[n, i] = rate * weights[n]
        keep_ref[i] = jnp.where(inside, 1.0 - rate * (weight_sum + mass), 0.0)
        couple_ref[i] = 0.25 * rate * mass
        rate_ref[i] = rate

    for i in range(EXT_X - 2):
        one(i)


def relax_and_gather(
    side_ref,
    start_ref,
    weight_s,
    keep_s,
    couple_s,
    rate_ref,
    ext_ref,
    z_ref,
    stiff_ref,
    where_ref,
    ids_ref,
    out_ref,
    message_ref,
    first_s,
    second_s,
    push_s,
    pieces_s,
):
    beyond = unpack_z(side_ref[0], z_ref)
    for c in range(3):
        push_s[c, :, :, :LANES] = rate_ref[:, :, :LANES] * ext_ref[c]
        push_s[c, :, :, LANES:] = rate_ref[:, :, LANES:] * beyond(c)

    def sweep(source, target, lowest, highest):
        def one(x):
            i = x - 1
            gathered = [around(lambda y, c=c: source[c, y], x) for c in range(3)]
            shared = couple_s[i] * (gathered[0][0] + gathered[1][0] + gathered[2][0])
            for c in range(3):
                middle, others = gathered[c]
                value = keep_s[i] * middle + (push_s[c, i] - shared)
                for n in range(6):
                    value = value + weight_s[n, i] * others[n]
                target[c, x] = value

        for x in range(lowest, highest):
            one(x)

    sweep(start_ref, second_s, 1, EXT_X - 1)
    sweep(second_s, first_s, 2, EXT_X - 2)

    def finish(x):
        i = x - 1
        middles = [first_s[c, x, :CY, :LANES] for c in range(3)]
        shared = couple_s[i, :CY, :LANES] * (middles[0] + middles[1] + middles[2])
        for c in range(3):
            columns = first_s[c, x, :, :LANES]
            halo = first_s[c, x, :CY, LANES:]
            others = (
                first_s[c, x + 1, :CY, :LANES],
                first_s[c, x - 1, :CY, :LANES],
                pltpu.roll(columns, EXT_Y - 1, 0)[:CY],
                pltpu.roll(columns, 1, 0)[:CY],
                pltpu.roll(jnp.where(last_lane == 0, halo, middles[c]), LANES - 1, 1),
                pltpu.roll(jnp.where(last_lane == LANES - 1, halo, middles[c]), 1, 1),
            )
            value = keep_s[i, :CY, :LANES] * middles[c] + (push_s[c, i, :CY, :LANES] - shared)
            for n in range(6):
                value = value + weight_s[n, i, :CY, :LANES] * others[n]
            out_ref[c, x - 3] = value

    last_lane = iota((CY, LANES), 1)
    for x in range(3, 3 + CX):
        finish(x)

    own_rows = CX * CY
    for c in range(3):
        scaled = (out_ref[c] * stiff_ref[...]).reshape(own_rows, LANES)
        for n, piece in enumerate(halves(scaled)):
            pieces_s[c * own_rows : (c + 1) * own_rows, n * LANES : (n + 1) * LANES] = piece.astype(bf16)
    count = HULL_DESTS * HULL_ROWS
    row_number = iota((own_rows, LANES), 0)
    lane_number = iota((LANES, LANES), 0)
    group = 2 * HULL_ROWS
    for g in range(count // group):
        chosen = []
        for r in range(g * group, (g + 1) * group):
            chosen.append(jnp.where(lane_number == where_ref[count + r : count + r + 1, :], 1.0, 0.0).astype(bf16))
        chosen = jnp.concatenate(chosen, axis=1)
        found = jnp.dot(pieces_s[...], jnp.concatenate([chosen, chosen], axis=0), preferred_element_type=f32)
        for i in range(group):
            r = g * group + i
            here = row_number == where_ref[r : r + 1, :]
            base = r // HULL_ROWS * 4 * HULL_ROWS + r % HULL_ROWS
            for c in range(3):
                part = found[c * own_rows : (c + 1) * own_rows, i * LANES : (i + 1) * LANES]
                spot = base + c * HULL_ROWS
                message_ref[spot : spot + 1, :] = jnp.sum(jnp.where(here, part, 0.0), axis=0, keepdims=True)
            spot = base + 3 * HULL_ROWS
            message_ref[spot : spot + 1, :] = ids_ref[r : r + 1, :]


def scatter_hull(nodes_ref, out_hbm, overflow_ref, out_ref, sem):
    flags = nodes_ref[pl.ds(4 * HULL_ROWS - 1, HULL_DESTS, stride=4 * HULL_ROWS), :]
    last = iota((HULL_DESTS, LANES), 1) == LANES - 1
    overflow_ref[0] = jnp.max(jnp.where(last, flags, 0.0)).astype(i32)
    row_number = iota((64, LANES), 0)
    column_number = iota((256, LANES), 0)
    sums = jnp.zeros((6 * 64, 256), f32)
    batch = 4
    for first in range(0, HULL_DESTS, batch):
        lefts, rights = [], []
        for n in range(batch * HULL_ROWS):
            base = (first + n // HULL_ROWS) * 4 * HULL_ROWS + n % HULL_ROWS
            ids = nodes_ref[base + 3 * HULL_ROWS : base + 3 * HULL_ROWS + 1, :].astype(i32) - 1
            here = row_number == (ids >> 8)
            pieces = []
            for c in range(3):
                values = nodes_ref[base + c * HULL_ROWS : base + c * HULL_ROWS + 1, :]
                pieces.extend(jnp.where(here, part, 0.0).astype(bf16) for part in halves(values))
            lefts.append(jnp.concatenate(pieces, axis=0))
            rights.append(jnp.where(column_number == (ids & 255), 1.0, 0.0).astype(bf16))
        sums = sums + dot_last(jnp.concatenate(lefts, axis=1), jnp.concatenate(rights, axis=1))
    for c in range(3):
        out_ref[c] = sums[2 * c * 64 : (2 * c + 1) * 64] + sums[(2 * c + 1) * 64 : (2 * c + 2) * 64]
    copy = pltpu.make_async_copy(out_ref, out_hbm, sem)
    copy.start()
    copy.wait()


def shaped(*shape, dtype=f32):
    return jax.ShapeDtypeStruct(shape, dtype)


def call(kernel, outs, scratch, cost, *args, places="", out_places=""):
    spaces = {"V": pltpu.VMEM, "S": pltpu.SMEM, "H": pltpu.HBM}

    def specs(count, names):
        names = names + "V" * (count - len(names))
        return [pl.BlockSpec(memory_space=spaces[name]) for name in names]

    args = [pltpu.with_memory_space_constraint(arg, pltpu.HBM) if place == "H" else arg for arg, place in zip(args, places + "V" * len(args))]
    if isinstance(outs, tuple):
        outs = tuple(pltpu.HBM(out.shape, out.dtype) if place == "H" else out for out, place in zip(outs, out_places + "V" * len(outs)))
    return pl.pallas_call(
        kernel,
        out_shape=outs,
        in_specs=specs(len(args), places),
        out_specs=tuple(specs(len(outs), out_places)) if isinstance(outs, tuple) else specs(1, out_places)[0],
        scratch_shapes=scratch,
        compiler_params=PARAMS,
        cost_estimate=pl.CostEstimate(flops=cost, bytes_accessed=1 << 20, transcendentals=0),
        name=getattr(kernel, "func", kernel).__name__,
    )(*args)


def pair_exchange(axis, even, odd):
    count = lax.axis_size(axis)
    results = []
    for first, values in ((0, even), (1, odd)):
        pairs = [(i, (i + 1) % count) for i in range(first, count, 2)]
        results.append(lax.ppermute(values, axis, pairs + [(b, a) for a, b in pairs]))
    return results


def per_device(start_field, stiffness, mass, sens_values, sens_cells, sens_counts, hull_cells, hull_patches):
    slabs = shaped(14, CY, CZ)
    gx, gy, side = (lax.axis_index(axis).astype(i32).reshape(1) for axis in ("gx", "gy", "gz"))
    packed, even, odd = call(
        pack_slots,
        (shaped(3 * BLOCKS, LANES), slabs, slabs),
        [
            pltpu.VMEM((3, SLOT_ROWS, LANES), f32),
            pltpu.VMEM((SLOT_ROWS, LANES), i32),
            pltpu.VMEM((1, BLOCKS), i32),
            pltpu.SemaphoreType.DMA((13,)),
        ],
        1 << 20,
        gx,
        sens_values.reshape(3, SLOT_ROWS, LANES),
        sens_cells.reshape(SLOT_ROWS, LANES),
        sens_counts.reshape(1, BLOCKS),
        start_field,
        stiffness,
        mass,
        places="SHHHHHH",
    )
    packed = packed.reshape(BLOCKS, 1, 3 * LANES)
    arrived = lax.all_to_all(packed, ("gx", "gy"), split_axis=0, concat_axis=0, tiled=True)
    xeven, xodd = pair_exchange("gx", even, odd)
    count = HULL_DESTS * HULL_ROWS
    where, ids = call(
        route_hull,
        (shaped(2 * count, LANES, dtype=i32), shaped(count, LANES)),
        [pltpu.VMEM((4 * count, SLOTS), bf16), pltpu.VMEM((LANES, SLOTS), bf16)],
        1 << 31,
        hull_cells.reshape(SLOT_ROWS, LANES),
        hull_patches.reshape(SLOT_ROWS, LANES),
    )
    n_gx, n_gy = lax.axis_size("gx"), lax.axis_size("gy")
    y_message = shaped(CX + 4, Y_ROWS, CZ)
    even, odd = call(
        functools.partial(pack_y, n_gx),
        (y_message, y_message),
        [pltpu.VMEM((5, 2, CX, 8, CZ), f32), pltpu.SemaphoreType.DMA((10,))],
        1 << 34,
        gx,
        gy,
        start_field,
        stiffness,
        mass,
        xeven,
        xodd,
        places="SSHHH",
    )
    yeven, yodd = pair_exchange("gy", even, odd)
    arrived, yeven, yodd = lax.optimization_barrier((arrived, yeven, yodd))
    y_message = shaped(CX + 4, 6, CZ)
    source, even, odd = call(
        scatter_slots,
        (shaped(3, CX + 4, CY, CZ), y_message, y_message),
        [],
        1 << 32,
        gy,
        arrived.reshape(3 * BLOCKS, LANES),
        places="S",
    )
    rows = (EXT_X - 2) * EXT_Y
    z_message = shaped(Z_ROWS, rows)
    source_even, source_odd = pair_exchange("gy", even, odd)
    ext, faces = call(
        functools.partial(widen_fixed, n_gx, n_gy),
        (shaped(5, EXT_X, EXT_Y, CZ), z_message),
        [],
        1 << 20,
        gx,
        gy,
        side,
        start_field,
        stiffness,
        mass,
        xeven,
        xodd,
        yeven,
        yodd,
        places="SSS",
    )
    faces = lax.ppermute(faces, "gz", [(0, 1), (1, 0)])
    source_ext, source_faces = call(
        functools.partial(widen_source, n_gy),
        (shaped(3, EXT_X - 2, EXT_Y, CZ), z_message),
        [],
        1 << 20,
        gy,
        side,
        source,
        source_even,
        source_odd,
        places="SS",
    )
    source_faces = lax.ppermute(source_faces, "gz", [(0, 1), (1, 0)])
    wide = (EXT_X - 2, EXT_Y, 2 * CZ)
    full = (EXT_X, EXT_Y, 2 * CZ)
    prepared = call(
        prepare,
        (shaped(3, *full), shaped(6, *wide), shaped(*wide), shaped(*wide), shaped(*wide)),
        [pltpu.VMEM(full, f32), pltpu.VMEM(wide, f32)],
        1 << 30,
        side,
        ext,
        faces,
        places="S",
    )
    field, outgoing = call(
        relax_and_gather,
        (shaped(3, CX, CY, CZ), shaped(4 * count, LANES)),
        [
            pltpu.VMEM((3,) + full, f32),
            pltpu.VMEM((3,) + full, f32),
            pltpu.VMEM((3,) + wide, f32),
            pltpu.VMEM((3 * CX * CY, 2 * LANES), bf16),
        ],
        1 << 32,
        side,
        *prepared,
        source_ext,
        source_faces,
        stiffness,
        where,
        ids,
        places="S",
    )
    outgoing = outgoing.reshape(HULL_DESTS, 1, 4 * HULL_ROWS * LANES)
    nodes = lax.all_to_all(outgoing, ("gy", "gz"), split_axis=0, concat_axis=0, tiled=True)
    nodes = nodes.reshape(4 * count, LANES)
    patch, overflow = call(
        scatter_hull,
        (shaped(3, 64, 256), shaped(1, dtype=i32)),
        [pltpu.VMEM((3, 64, 256), f32), pltpu.SemaphoreType.DMA],
        1 << 32,
        nodes,
        out_places="HS",
    )

    def in_messages():
        return patch

    def every_node():
        cells = hull_cells[0, 0]
        values = field.reshape(3, -1)[:, cells] * stiffness.reshape(-1)[cells]
        sent = jnp.concatenate([values, hull_patches[0].astype(f32)], axis=0)
        sent = jnp.broadcast_to(sent[None], (HULL_DESTS,) + sent.shape)
        got = lax.all_to_all(sent, ("gy", "gz"), split_axis=0, concat_axis=0, tiled=True)
        got = jnp.swapaxes(got, 0, 1).reshape(4, -1)
        spots = got[3].astype(i32) - lax.axis_index(("gy", "gz")) * PATCH_BLOCK
        mine = (spots >= 0) & (spots < PATCH_BLOCK)
        added = jnp.where(mine, got[:3], 0.0)
        patch = jnp.zeros((3, PATCH_BLOCK), f32).at[:, jnp.where(mine, spots, 0)].add(added)
        return patch.reshape(3, 64, 256)

    patch = lax.cond(overflow[0] > 0, every_node, in_messages)
    return field, patch


def solution(mesh):
    placed = (
        P(None, "gx", "gy", "gz"),
        P("gx", "gy", "gz"),
        P("gx", "gy", "gz"),
        P(None, "gz", ("gx", "gy"), None),
        P("gz", ("gx", "gy"), None),
        P("gz", ("gx", "gy"), None),
        P("gx", ("gy", "gz"), None),
        P("gx", ("gy", "gz"), None),
    )
    return jax.shard_map(
        per_device,
        mesh=mesh,
        in_specs=placed,
        out_specs=(P(None, "gx", "gy", "gz"), P(None, ("gy", "gz"), "gx")),
        check_vma=False,
    )
```

```python
import functools

import jax
import jax.numpy as jnp
from jax import lax
from jax.experimental import pallas as pl
from jax.experimental.pallas import tpu as pltpu
from jax.sharding import PartitionSpec as P

CX, CY, CZ = 8, 24, 128
LANES = 128
SLOTS = 4096
SLOT_ROWS = SLOTS // LANES
BLOCKS = 128
CAP = 32
HULL_DESTS = 16
PATCH_BLOCK = 64 * 256
HULL_ROWS = 3
HULL_CAP = HULL_ROWS * LANES - 1
Y_ROWS = 14
Y_FIELDS = ((0, 3), (3, 3), (6, 3), (9, 3), (12, 2))
Z_ROWS = 16
EXT_X = CX + 6
EXT_Y = 32
RELAX = 0.8

f32, bf16, i32 = jnp.float32, jnp.bfloat16, jnp.int32
PARAMS = pltpu.CompilerParams(vmem_limit_bytes=24 * 1024 * 1024)


def iota(shape, dim):
    return lax.broadcasted_iota(i32, shape, dim)


def halves(values):
    high = values.astype(bf16).astype(f32)
    return high, values - high


def dot_last(a, b):
    return lax.dot_general(a, b, (((1,), (1,)), ((), ())), preferred_element_type=f32)


def by_parity(place, even, odd):
    index, count = place
    is_odd = lax.rem(index, 2) == 1
    low = jnp.where(is_odd, even, odd) * jnp.where(index > 0, 1.0, 0.0)
    high = jnp.where(is_odd, odd, even) * jnp.where(index < count - 1, 1.0, 0.0)
    return low, high


def pack_slots(
    gx_ref, values_hbm, cells_hbm, counts_hbm, field_hbm, stiff_hbm, mass_hbm, out_ref, even_ref, odd_ref, values_ref, cells_ref, counts_ref, sems
):
    copies = [
        pltpu.make_async_copy(values_hbm, values_ref, sems.at[0]),
        pltpu.make_async_copy(cells_hbm, cells_ref, sems.at[1]),
        pltpu.make_async_copy(counts_hbm, counts_ref, sems.at[2]),
    ]
    odd = lax.rem(gx_ref[0], 2)
    for slab, up in ((even_ref, 1 - odd), (odd_ref, odd)):
        planes, mass_planes = pl.ds(up * (CX - 3), 3), pl.ds(up * (CX - 2), 2)
        for c in range(3):
            copies.append(pltpu.make_async_copy(field_hbm.at[c, planes], slab.at[pl.ds(3 * c, 3)], sems.at[len(copies)]))
        copies.append(pltpu.make_async_copy(stiff_hbm.at[planes], slab.at[pl.ds(9, 3)], sems.at[len(copies)]))
        copies.append(pltpu.make_async_copy(mass_hbm.at[mass_planes], slab.at[pl.ds(12, 2)], sems.at[len(copies)]))
    for copy in copies:
        copy.start()
    for copy in copies[:3]:
        copy.wait()
    counts = counts_ref[...].astype(f32)
    spread = jnp.where(iota((SLOT_ROWS, BLOCKS), 1) // 4 == iota((SLOT_ROWS, BLOCKS), 0), counts, 0.0)
    place = jnp.where(iota((BLOCKS, LANES), 0) % 4 == iota((BLOCKS, LANES), 1) // CAP, 1.0, 0.0)
    limits = jnp.dot(spread.astype(bf16), place.astype(bf16), preferred_element_type=f32)
    lane = iota((SLOT_ROWS, LANES), 1)
    live = (lane % CAP).astype(f32) < limits
    parts = [jnp.where(live, values_ref[c], 0.0) for c in range(3)] + [cells_ref[...].astype(f32)]
    quarter = lane // CAP
    row = iota((SLOT_ROWS, LANES), 0)
    for q in range(4):
        message = jnp.zeros((SLOT_ROWS, LANES), f32)
        for c in range(4):
            turned = parts[c] if c == q else pltpu.roll(parts[c], (c - q) * CAP % LANES, 1)
            message = jnp.where(quarter == c, turned, message)
        below = jnp.where(row >= 2, pltpu.roll(message, 2, 0), 0.0)
        above = jnp.where(row < SLOT_ROWS - 2, pltpu.roll(message, SLOT_ROWS - 2, 0), 0.0)
        out_ref[pl.ds(3 * q, SLOT_ROWS, stride=12), :] = below
        out_ref[pl.ds(3 * q + 1, SLOT_ROWS, stride=12), :] = message
        out_ref[pl.ds(3 * q + 2, SLOT_ROWS, stride=12), :] = above
    for copy in copies[3:]:
        copy.wait()


def scatter_slots(gy_ref, slots_ref, source_ref, even_ref, odd_ref):
    lane = iota((SLOT_ROWS, LANES), 1)
    quarter = lane // CAP
    own_rows = CY * CX
    side_rows = CY * 2

    def unpack(k):
        parts = [jnp.zeros((SLOT_ROWS, LANES), f32) for _ in range(4)]
        for q in range(4):
            message = slots_ref[pl.ds(3 * q + k, SLOT_ROWS, stride=12), :]
            for c in range(4):
                turned = message if c == q else pltpu.roll(message, (q - c) * CAP % LANES, 1)
                parts[c] = jnp.where(quarter == q, turned, parts[c])
        ids = parts[3].astype(i32)
        pieces = []
        for c in range(3):
            pieces.extend(halves(parts[c]))
        return ids // LANES, ids % LANES, pieces

    lane_number = iota((LANES, LANES), 0)
    row_number = iota((2 * LANES, LANES), 0)
    side_number = iota((side_rows, LANES), 0)
    batch = 8
    rows, lanes, pieces = unpack(1)
    sums = jnp.zeros((6 * LANES, 2 * LANES), f32)
    for start in range(0, SLOT_ROWS, batch):
        lefts, rights = [], []
        for r in range(start, start + batch):
            here = lane_number == lanes[r : r + 1, :]
            lefts.append(jnp.concatenate([jnp.where(here, piece[r : r + 1, :], 0.0).astype(bf16) for piece in pieces], axis=0))
            rights.append(jnp.where(row_number == rows[r : r + 1, :], 1.0, 0.0).astype(bf16))
        sums = sums + dot_last(jnp.concatenate(lefts, axis=1), jnp.concatenate(rights, axis=1))
    for c in range(3):
        one = sums[2 * c * LANES : (2 * c + 1) * LANES] + sums[(2 * c + 1) * LANES : (2 * c + 2) * LANES]
        source_ref[c, 2 : 2 + CX] = jnp.transpose(one)[:own_rows].reshape(CX, CY, LANES)
    for k, first, target in ((0, own_rows - side_rows, 0), (2, 0, 2 + CX)):
        rows, lanes, pieces = unpack(k)
        sums = jnp.zeros((6 * side_rows, LANES), f32)
        for start in range(0, SLOT_ROWS, batch):
            lefts, rights = [], []
            for r in range(start, start + batch):
                here = side_number == rows[r : r + 1, :] - first
                lefts.append(jnp.concatenate([jnp.where(here, piece[r : r + 1, :], 0.0).astype(bf16) for piece in pieces], axis=0))
                rights.append(jnp.where(lane_number == lanes[r : r + 1, :], 1.0, 0.0).astype(bf16))
            sums = sums + dot_last(jnp.concatenate(lefts, axis=1), jnp.concatenate(rights, axis=1))
        for c in range(3):
            one = sums[2 * c * side_rows : (2 * c + 1) * side_rows] + sums[(2 * c + 1) * side_rows : (2 * c + 2) * side_rows]
            source_ref[c, target : target + 2] = one.reshape(2, CY, LANES)
    is_odd = lax.rem(gy_ref[0], 2) == 1
    for c in range(3):
        here = slice(2 * c, 2 * c + 2)
        first, last = source_ref[c, :, 0:2, :], source_ref[c, :, CY - 2 :, :]
        even_ref[:, here, :] = jnp.where(is_odd, first, last)
        odd_ref[:, here, :] = jnp.where(is_odd, last, first)


def pack_y(n_gx, gx_ref, gy_ref, field_hbm, stiff_hbm, mass_hbm, xeven_ref, xodd_ref, even_ref, odd_ref, ends_ref, sems):
    copies = []
    for number in range(5):
        own = field_hbm.at[number] if number < 3 else (stiff_hbm if number == 3 else mass_hbm)
        for n, rows in enumerate((pl.ds(0, 8), pl.ds(CY - 8, 8))):
            copies.append(pltpu.make_async_copy(own.at[:, rows], ends_ref.at[number, n], sems.at[len(copies)]))
    for copy in copies:
        copy.start()
    for copy in copies:
        copy.wait()
    is_odd = lax.rem(gy_ref[0], 2) == 1
    for number, (start, width) in enumerate(Y_FIELDS):
        here = slice(start, start + width)
        planes = slice(3 * number, 3 * number + 3) if number < 4 else slice(12, 14)
        pieces = [[], []]
        for n, (rows, own_rows) in enumerate(((slice(0, width), slice(0, width)), (slice(CY - width, CY), slice(8 - width, 8)))):
            low, high = by_parity((gx_ref[0], n_gx), xeven_ref[planes, rows, :], xodd_ref[planes, rows, :])
            own = ends_ref[number, n, :, own_rows, :]
            pieces[n].extend([(slice(0, 2), low[-2:]), (slice(2, 2 + CX), own), (slice(2 + CX, CX + 4), high[:2])])
        for (where, first), (_, last) in zip(*pieces):
            even_ref[where, here, :] = jnp.where(is_odd, first, last)
            odd_ref[where, here, :] = jnp.where(is_odd, last, first)


def route_hull(cells_ref, patches_ref, where_ref, ids_ref, rows_s, lanes_s):
    patches = patches_ref[...]
    cells = cells_ref[...]
    dest = patches // PATCH_BLOCK
    local = patches % PATCH_BLOCK
    hits = [jnp.where(dest == d, 1.0, 0.0) for d in range(HULL_DESTS)]
    stacked = jnp.concatenate(hits, axis=0).astype(bf16)
    upto = jnp.where(iota((LANES, LANES), 0) <= iota((LANES, LANES), 1), 1.0, 0.0).astype(bf16)
    total = HULL_DESTS * SLOT_ROWS
    within = jnp.dot(stacked, upto, preferred_element_type=f32)
    row_sums = jnp.dot(stacked, jnp.ones((LANES, LANES), bf16), preferred_element_type=f32)
    a, b = iota((total, total), 0), iota((total, total), 1)
    earlier = jnp.where((a // SLOT_ROWS == b // SLOT_ROWS) & (b < a), 1.0, 0.0).astype(bf16)
    offsets = jnp.dot(earlier, row_sums.astype(bf16), preferred_element_type=f32)
    rank = jnp.zeros((SLOT_ROWS, LANES), f32)
    for d in range(HULL_DESTS):
        cut = slice(d * SLOT_ROWS, (d + 1) * SLOT_ROWS)
        rank = rank + hits[d] * (within[cut] + offsets[cut] - 1.0)
    rank = rank.astype(i32)
    overflow = jnp.max(jnp.where(rank >= HULL_CAP, 1.0, 0.0))
    slot_row = jnp.where(rank < HULL_CAP, dest * HULL_ROWS + rank // LANES, -1)
    slot_lane = rank % LANES
    payload = [cells // LANES, cells % LANES, local // 256 + 1, local % 256]
    payload = [p.astype(f32) for p in payload]
    count = HULL_DESTS * HULL_ROWS
    row_number = iota((count, LANES), 0)
    lane_number = iota((LANES, LANES), 0)
    for r in range(SLOT_ROWS):
        cut = slice(r * LANES, (r + 1) * LANES)
        here = row_number == slot_row[r : r + 1, :]
        for n in range(4):
            rows_s[n * count : (n + 1) * count, cut] = jnp.where(here, payload[n][r : r + 1, :], 0.0).astype(bf16)
        lanes_s[:, cut] = jnp.where(lane_number == slot_lane[r : r + 1, :], 1.0, 0.0).astype(bf16)
    placed = dot_last(rows_s[...], lanes_s[...])
    where_ref[...] = placed[: 2 * count].astype(i32)
    ids = jnp.maximum((placed[2 * count : 3 * count] - 1.0) * 256.0 + placed[3 * count :] + 1.0, 0.0)
    last = (iota((count, LANES), 1) == LANES - 1) & (row_number % HULL_ROWS == HULL_ROWS - 1)
    ids_ref[...] = jnp.where(last, overflow, ids)


def pack_z(side, arrays, z_ref):
    lane = iota((1, 1, LANES), 2)
    total = jnp.zeros((EXT_X - 2, EXT_Y, LANES), f32)
    for number, array in enumerate(arrays):
        shift = jnp.where(side == 0, (3 * number + 3) % LANES, 3 * number)
        turned = pltpu.roll(array.reshape((EXT_X - 2) * EXT_Y, LANES), shift, 1).reshape(EXT_X - 2, EXT_Y, LANES)
        total = jnp.where((lane >= 3 * number) & (lane < 3 * number + 3), turned, total)
    z_ref[...] = jnp.transpose(total.reshape((EXT_X - 2) * EXT_Y, LANES))[:Z_ROWS]


def unpack_z(side, z_ref):
    rows = (EXT_X - 2) * EXT_Y
    lane = iota((1, 1, LANES), 2)
    columns = jnp.transpose(jnp.concatenate([z_ref[...], jnp.zeros((LANES - Z_ROWS, rows), f32)], axis=0))
    first_lane = jnp.where(side == 0, 0, LANES - 3)
    near = (lane >= first_lane) & (lane < first_lane + 3)

    def beyond(number):
        shift = jnp.where(side == 0, (LANES - 3 * number) % LANES, (2 * LANES - 3 - 3 * number) % LANES)
        return jnp.where(near, pltpu.roll(columns, shift, 1).reshape(EXT_X - 2, EXT_Y, LANES), 0.0)

    return beyond


def widen_fixed(n_gx, n_gy, gx_ref, gy_ref, side_ref, field_ref, stiff_ref, mass_ref, xeven_ref, xodd_ref, yeven_ref, yodd_ref, ext_ref, z_ref):
    zeros = jnp.zeros((EXT_X, EXT_Y - CY, LANES), f32)
    for number, (start, width) in enumerate(Y_FIELDS):
        target = ext_ref.at[number]
        target[:, CY:, :] = zeros
        planes = slice(3 * number, 3 * number + 3) if number < 4 else slice(12, 14)
        low, high = by_parity((gx_ref[0], n_gx), xeven_ref[planes], xodd_ref[planes])
        own = field_ref.at[number] if number < 3 else (stiff_ref if number == 3 else mass_ref)
        if width < 3:
            target[0, :CY, :] = jnp.zeros((CY, LANES), f32)
            target[EXT_X - 1, :CY, :] = jnp.zeros((CY, LANES), f32)
        target[3 - width : 3, :CY, :] = low
        target[3 : 3 + CX, :CY, :] = own[...]
        target[3 + CX : 3 + CX + width, :CY, :] = high
        here = slice(start, start + width)
        low, high = by_parity((gy_ref[0], n_gy), yeven_ref[:, here, :], yodd_ref[:, here, :])
        target[1 : EXT_X - 1, CY : CY + width, :] = high
        target[1 : EXT_X - 1, EXT_Y - width :, :] = low
    pack_z(side_ref[0], [ext_ref[number, 1 : EXT_X - 1] for number in range(5)], z_ref)


def widen_source(n_gy, gy_ref, side_ref, source_ref, yeven_ref, yodd_ref, ext_ref, z_ref):
    zeros = jnp.zeros((EXT_X - 2, EXT_Y - CY, LANES), f32)
    for c in range(3):
        here = slice(2 * c, 2 * c + 2)
        low, high = by_parity((gy_ref[0], n_gy), yeven_ref[:, here, :], yodd_ref[:, here, :])
        ext_ref[c, :, CY:, :] = zeros
        ext_ref[c, :, :CY, :] = source_ref[c]
        ext_ref[c, :, CY : CY + 2, :] = high
        ext_ref[c, :, EXT_Y - 2 :, :] = low
    pack_z(side_ref[0], [ext_ref[c] for c in range(3)], z_ref)


def around(ref_at, x):
    middle = ref_at(x)
    return middle, (
        ref_at(x + 1),
        ref_at(x - 1),
        pltpu.roll(middle, EXT_Y - 1, 0),
        pltpu.roll(middle, 1, 0),
        pltpu.roll(middle, 2 * LANES - 1, 1),
        pltpu.roll(middle, 1, 1),
    )


def prepare(side_ref, ext_ref, z_ref, start_ref, weight_ref, keep_ref, couple_ref, rate_ref, stiff_s, mass_s):
    beyond = unpack_z(side_ref[0], z_ref)
    empty = jnp.zeros((EXT_Y, LANES), f32)
    for c in range(3):
        start_ref[c, :, :, :LANES] = ext_ref[c]
        start_ref[c, 1 : EXT_X - 1, :, LANES:] = beyond(c)
        start_ref[c, 0, :, LANES:] = empty
        start_ref[c, EXT_X - 1, :, LANES:] = empty
    stiff_s[:, :, :LANES] = ext_ref[3]
    stiff_s[1 : EXT_X - 1, :, LANES:] = beyond(3)
    stiff_s[0, :, LANES:] = empty
    stiff_s[EXT_X - 1, :, LANES:] = empty
    mass_s[:, :, :LANES] = ext_ref[4, 1 : EXT_X - 1]
    mass_s[:, :, LANES:] = beyond(4)

    def one(i):
        middle, others = around(lambda x: stiff_s[x], i + 1)
        weights = [0.5 * (middle + other) for other in others]
        weight_sum = weights[0] + weights[1] + weights[2] + weights[3] + weights[4] + weights[5]
        mass = mass_s[i]
        inside = middle > 0.0
        rate = jnp.where(inside, RELAX / jnp.where(inside, weight_sum + 1.25 * mass, 1.0), 0.0)
        for n in range(6):
            weight_ref[n, i] = rate * weights[n]
        keep_ref[i] = jnp.where(inside, 1.0 - rate * (weight_sum + mass), 0.0)
        couple_ref[i] = 0.25 * rate * mass
        rate_ref[i] = rate

    for i in range(EXT_X - 2):
        one(i)


def relax_and_gather(
    side_ref,
    start_ref,
    weight_s,
    keep_s,
    couple_s,
    rate_ref,
    ext_ref,
    z_ref,
    stiff_ref,
    where_ref,
    ids_ref,
    out_ref,
    message_ref,
    first_s,
    second_s,
    push_s,
    pieces_s,
):
    beyond = unpack_z(side_ref[0], z_ref)
    for c in range(3):
        push_s[c, :, :, :LANES] = rate_ref[:, :, :LANES] * ext_ref[c]
        push_s[c, :, :, LANES:] = rate_ref[:, :, LANES:] * beyond(c)

    def sweep(source, target, lowest, highest):
        def one(x):
            i = x - 1
            gathered = [around(lambda y, c=c: source[c, y], x) for c in range(3)]
            shared = couple_s[i] * (gathered[0][0] + gathered[1][0] + gathered[2][0])
            for c in range(3):
                middle, others = gathered[c]
                value = keep_s[i] * middle + (push_s[c, i] - shared)
                for n in range(6):
                    value = value + weight_s[n, i] * others[n]
                target[c, x] = value

        for x in range(lowest, highest):
            one(x)

    sweep(start_ref, second_s, 1, EXT_X - 1)
    sweep(second_s, first_s, 2, EXT_X - 2)

    def finish(x):
        i = x - 1
        middles = [first_s[c, x, :CY, :LANES] for c in range(3)]
        shared = couple_s[i, :CY, :LANES] * (middles[0] + middles[1] + middles[2])
        for c in range(3):
            columns = first_s[c, x, :, :LANES]
            halo = first_s[c, x, :CY, LANES:]
            others = (
                first_s[c, x + 1, :CY, :LANES],
                first_s[c, x - 1, :CY, :LANES],
                pltpu.roll(columns, EXT_Y - 1, 0)[:CY],
                pltpu.roll(columns, 1, 0)[:CY],
                pltpu.roll(jnp.where(last_lane == 0, halo, middles[c]), LANES - 1, 1),
                pltpu.roll(jnp.where(last_lane == LANES - 1, halo, middles[c]), 1, 1),
            )
            value = keep_s[i, :CY, :LANES] * middles[c] + (push_s[c, i, :CY, :LANES] - shared)
            for n in range(6):
                value = value + weight_s[n, i, :CY, :LANES] * others[n]
            out_ref[c, x - 3] = value

    last_lane = iota((CY, LANES), 1)
    for x in range(3, 3 + CX):
        finish(x)

    own_rows = CX * CY
    for c in range(3):
        scaled = (out_ref[c] * stiff_ref[...]).reshape(own_rows, LANES)
        for n, piece in enumerate(halves(scaled)):
            pieces_s[c * own_rows : (c + 1) * own_rows, n * LANES : (n + 1) * LANES] = piece.astype(bf16)
    count = HULL_DESTS * HULL_ROWS
    row_number = iota((own_rows, LANES), 0)
    lane_number = iota((LANES, LANES), 0)
    group = 2 * HULL_ROWS
    for g in range(count // group):
        chosen = []
        for r in range(g * group, (g + 1) * group):
            chosen.append(jnp.where(lane_number == where_ref[count + r : count + r + 1, :], 1.0, 0.0).astype(bf16))
        chosen = jnp.concatenate(chosen, axis=1)
        found = jnp.dot(pieces_s[...], jnp.concatenate([chosen, chosen], axis=0), preferred_element_type=f32)
        for i in range(group):
            r = g * group + i
            here = row_number == where_ref[r : r + 1, :]
            base = r // HULL_ROWS * 4 * HULL_ROWS + r % HULL_ROWS
            for c in range(3):
                part = found[c * own_rows : (c + 1) * own_rows, i * LANES : (i + 1) * LANES]
                spot = base + c * HULL_ROWS
                message_ref[spot : spot + 1, :] = jnp.sum(jnp.where(here, part, 0.0), axis=0, keepdims=True)
            spot = base + 3 * HULL_ROWS
            message_ref[spot : spot + 1, :] = ids_ref[r : r + 1, :]


def scatter_hull(nodes_ref, out_hbm, overflow_ref, out_ref, sem):
    flags = nodes_ref[pl.ds(4 * HULL_ROWS - 1, HULL_DESTS, stride=4 * HULL_ROWS), :]
    last = iota((HULL_DESTS, LANES), 1) == LANES - 1
    overflow_ref[0] = jnp.max(jnp.where(last, flags, 0.0)).astype(i32)
    row_number = iota((64, LANES), 0)
    column_number = iota((256, LANES), 0)
    sums = jnp.zeros((6 * 64, 256), f32)
    batch = 4
    for first in range(0, HULL_DESTS, batch):
        lefts, rights = [], []
        for n in range(batch * HULL_ROWS):
            base = (first + n // HULL_ROWS) * 4 * HULL_ROWS + n % HULL_ROWS
            ids = nodes_ref[base + 3 * HULL_ROWS : base + 3 * HULL_ROWS + 1, :].astype(i32) - 1
            here = row_number == (ids >> 8)
            pieces = []
            for c in range(3):
                values = nodes_ref[base + c * HULL_ROWS : base + c * HULL_ROWS + 1, :]
                pieces.extend(jnp.where(here, part, 0.0).astype(bf16) for part in halves(values))
            lefts.append(jnp.concatenate(pieces, axis=0))
            rights.append(jnp.where(column_number == (ids & 255), 1.0, 0.0).astype(bf16))
        sums = sums + dot_last(jnp.concatenate(lefts, axis=1), jnp.concatenate(rights, axis=1))
    for c in range(3):
        out_ref[c] = sums[2 * c * 64 : (2 * c + 1) * 64] + sums[(2 * c + 1) * 64 : (2 * c + 2) * 64]
    copy = pltpu.make_async_copy(out_ref, out_hbm, sem)
    copy.start()
    copy.wait()


def shaped(*shape, dtype=f32):
    return jax.ShapeDtypeStruct(shape, dtype)


def call(kernel, outs, scratch, cost, *args, places="", out_places=""):
    spaces = {"V": pltpu.VMEM, "S": pltpu.SMEM, "H": pltpu.HBM}

    def specs(count, names):
        names = names + "V" * (count - len(names))
        return [pl.BlockSpec(memory_space=spaces[name]) for name in names]

    args = [pltpu.with_memory_space_constraint(arg, pltpu.HBM) if place == "H" else arg for arg, place in zip(args, places + "V" * len(args))]
    if isinstance(outs, tuple):
        outs = tuple(pltpu.HBM(out.shape, out.dtype) if place == "H" else out for out, place in zip(outs, out_places + "V" * len(outs)))
    return pl.pallas_call(
        kernel,
        out_shape=outs,
        in_specs=specs(len(args), places),
        out_specs=tuple(specs(len(outs), out_places)) if isinstance(outs, tuple) else specs(1, out_places)[0],
        scratch_shapes=scratch,
        compiler_params=PARAMS,
        cost_estimate=pl.CostEstimate(flops=cost, bytes_accessed=1 << 20, transcendentals=0),
        name=getattr(kernel, "func", kernel).__name__,
    )(*args)


def pair_exchange(axis, even, odd):
    count = lax.axis_size(axis)
    results = []
    for first, values in ((0, even), (1, odd)):
        pairs = [(i, (i + 1) % count) for i in range(first, count, 2)]
        results.append(lax.ppermute(values, axis, pairs + [(b, a) for a, b in pairs]))
    return results


def per_device(start_field, stiffness, mass, sens_values, sens_cells, sens_counts, hull_cells, hull_patches):
    slabs = shaped(14, CY, CZ)
    gx, gy, side = (lax.axis_index(axis).astype(i32).reshape(1) for axis in ("gx", "gy", "gz"))
    packed, even, odd = call(
        pack_slots,
        (shaped(3 * BLOCKS, LANES), slabs, slabs),
        [
            pltpu.VMEM((3, SLOT_ROWS, LANES), f32),
            pltpu.VMEM((SLOT_ROWS, LANES), i32),
            pltpu.VMEM((1, BLOCKS), i32),
            pltpu.SemaphoreType.DMA((13,)),
        ],
        1 << 20,
        gx,
        sens_values.reshape(3, SLOT_ROWS, LANES),
        sens_cells.reshape(SLOT_ROWS, LANES),
        sens_counts.reshape(1, BLOCKS),
        start_field,
        stiffness,
        mass,
        places="SHHHHHH",
    )
    packed = packed.reshape(BLOCKS, 1, 3 * LANES)
    arrived = lax.all_to_all(packed, ("gx", "gy"), split_axis=0, concat_axis=0, tiled=True)
    xeven, xodd = pair_exchange("gx", even, odd)
    count = HULL_DESTS * HULL_ROWS
    where, ids = call(
        route_hull,
        (shaped(2 * count, LANES, dtype=i32), shaped(count, LANES)),
        [pltpu.VMEM((4 * count, SLOTS), bf16), pltpu.VMEM((LANES, SLOTS), bf16)],
        1 << 31,
        hull_cells.reshape(SLOT_ROWS, LANES),
        hull_patches.reshape(SLOT_ROWS, LANES),
    )
    n_gx, n_gy = lax.axis_size("gx"), lax.axis_size("gy")
    y_message = shaped(CX + 4, Y_ROWS, CZ)
    even, odd = call(
        functools.partial(pack_y, n_gx),
        (y_message, y_message),
        [pltpu.VMEM((5, 2, CX, 8, CZ), f32), pltpu.SemaphoreType.DMA((10,))],
        1 << 34,
        gx,
        gy,
        start_field,
        stiffness,
        mass,
        xeven,
        xodd,
        places="SSHHH",
    )
    yeven, yodd = pair_exchange("gy", even, odd)
    arrived, yeven, yodd, where, ids = lax.optimization_barrier((arrived, yeven, yodd, where, ids))
    y_message = shaped(CX + 4, 6, CZ)
    source, even, odd = call(
        scatter_slots,
        (shaped(3, CX + 4, CY, CZ), y_message, y_message),
        [],
        1 << 32,
        gy,
        arrived.reshape(3 * BLOCKS, LANES),
        places="S",
    )
    rows = (EXT_X - 2) * EXT_Y
    z_message = shaped(Z_ROWS, rows)
    source_even, source_odd = pair_exchange("gy", even, odd)
    ext, faces = call(
        functools.partial(widen_fixed, n_gx, n_gy),
        (shaped(5, EXT_X, EXT_Y, CZ), z_message),
        [],
        1 << 20,
        gx,
        gy,
        side,
        start_field,
        stiffness,
        mass,
        xeven,
        xodd,
        yeven,
        yodd,
        places="SSS",
    )
    faces = lax.ppermute(faces, "gz", [(0, 1), (1, 0)])
    source_ext, source_faces = call(
        functools.partial(widen_source, n_gy),
        (shaped(3, EXT_X - 2, EXT_Y, CZ), z_message),
        [],
        1 << 20,
        gy,
        side,
        source,
        source_even,
        source_odd,
        places="SS",
    )
    source_faces = lax.ppermute(source_faces, "gz", [(0, 1), (1, 0)])
    wide = (EXT_X - 2, EXT_Y, 2 * CZ)
    full = (EXT_X, EXT_Y, 2 * CZ)
    prepared = call(
        prepare,
        (shaped(3, *full), shaped(6, *wide), shaped(*wide), shaped(*wide), shaped(*wide)),
        [pltpu.VMEM(full, f32), pltpu.VMEM(wide, f32)],
        1 << 30,
        side,
        ext,
        faces,
        places="S",
    )
    field, outgoing = call(
        relax_and_gather,
        (shaped(3, CX, CY, CZ), shaped(4 * count, LANES)),
        [
            pltpu.VMEM((3,) + full, f32),
            pltpu.VMEM((3,) + full, f32),
            pltpu.VMEM((3,) + wide, f32),
            pltpu.VMEM((3 * CX * CY, 2 * LANES), bf16),
        ],
        1 << 32,
        side,
        *prepared,
        source_ext,
        source_faces,
        stiffness,
        where,
        ids,
        places="S",
    )
    outgoing = outgoing.reshape(HULL_DESTS, 1, 4 * HULL_ROWS * LANES)
    nodes = lax.all_to_all(outgoing, ("gy", "gz"), split_axis=0, concat_axis=0, tiled=True)
    nodes = nodes.reshape(4 * count, LANES)
    patch, overflow = call(
        scatter_hull,
        (shaped(3, 64, 256), shaped(1, dtype=i32)),
        [pltpu.VMEM((3, 64, 256), f32), pltpu.SemaphoreType.DMA],
        1 << 32,
        nodes,
        out_places="HS",
    )

    def in_messages():
        return patch

    def every_node():
        cells = hull_cells[0, 0]
        values = field.reshape(3, -1)[:, cells] * stiffness.reshape(-1)[cells]
        sent = jnp.concatenate([values, hull_patches[0].astype(f32)], axis=0)
        sent = jnp.broadcast_to(sent[None], (HULL_DESTS,) + sent.shape)
        got = lax.all_to_all(sent, ("gy", "gz"), split_axis=0, concat_axis=0, tiled=True)
        got = jnp.swapaxes(got, 0, 1).reshape(4, -1)
        spots = got[3].astype(i32) - lax.axis_index(("gy", "gz")) * PATCH_BLOCK
        mine = (spots >= 0) & (spots < PATCH_BLOCK)
        added = jnp.where(mine, got[:3], 0.0)
        patch = jnp.zeros((3, PATCH_BLOCK), f32).at[:, jnp.where(mine, spots, 0)].add(added)
        return patch.reshape(3, 64, 256)

    patch = lax.cond(overflow[0] > 0, every_node, in_messages)
    return field, patch


def solution(mesh):
    placed = (
        P(None, "gx", "gy", "gz"),
        P("gx", "gy", "gz"),
        P("gx", "gy", "gz"),
        P(None, "gz", ("gx", "gy"), None),
        P("gz", ("gx", "gy"), None),
        P("gz", ("gx", "gy"), None),
        P("gx", ("gy", "gz"), None),
        P("gx", ("gy", "gz"), None),
    )
    return jax.shard_map(
        per_device,
        mesh=mesh,
        in_specs=placed,
        out_specs=(P(None, "gx", "gy", "gz"), P(None, ("gy", "gz"), "gx")),
        check_vma=False,
    )
```
